32 devices in a mesh: gx: 8 (over z, y), gy: 4 (over x, core).
Axes of the slice: x: 2, y: 2, z: 4, core: 2. Of those that a mesh axis runs over, the one named last changes fastest.
Arguments:
- ocean_fields: bfloat16 [2048, 8, 512], P(('gx', 'gy')), may hold values from -6 to 6
- dest_device: int32 [2048, 2], P(('gx', 'gy')), may hold values from 0 to 31, all different within a row; in each aligned block of 64 rows (0 to 63, 64 to 127, ...) at most 8 rows name the same one
- dest_tile: int32 [2048, 2], P(('gx', 'gy')), may hold values from 0 to 7
- cell_target: int32 [2048, 2, 512], P(('gx', 'gy')), may hold values from 0 to 1023
- cell_weight: bfloat16 [2048, 2, 512], P(('gx', 'gy')), may hold values from 0.049804688 to 1
- sea_mask: int32 [2048, 512], P(('gx', 'gy')), may hold values 0 or 1
- land_flux: float32 [8, 256, 1024], P(None, 'gy', 'gx'), may hold values from -6 to 6
- land_area: float32 [256, 1024], P('gy', 'gx'), may hold values from 0.5 to 8
- kappa: float32 [256, 1024], P('gy', 'gx'), may hold values from 0.02 to 0.24
Outputs:
- smoothed: float32 [8, 256, 1024], P(None, 'gy', 'gx')
The draws below stay inside these ranges and needn't reach their ends.
Inputs may be any that keep to these rules, and one draw needn't show every extreme that they name: `dest_device`: the 2 devices named by one ocean tile differ; among the 64 ocean tiles of one device at most 8 name the same device.
All inputs are finite; a program needn't handle non-finite values. No bound on the sum of `sea_mask` on one device may be relied on, other than what follows from the above.
Results may differ from the reference program's by a relative error of at most 0.0003.
Values may be sent and summed in bfloat16 or wider, within the bound.
No kernel may reach another device: no remote copies, remote signals or barrier semaphores. Data moves between devices by JAX's collectives and lax.ppermute only.
A program may use at most 64 MiB of HBM per device.

```python
import math
import jax
import jax.numpy as jnp
import numpy as np

FIELDS = 8
INTERSECTIONS = 2
TILE_CELLS = 512
OCEAN_DEV = 64
TILE_ROWS = 8
ATM_COLS = 128
ATM_ROWS = 64
SWEEPS = 3
CAP = 8
ATM_TILES = 8
ATM_CELLS = 1024
OCEAN_TILES = 2048
GRID_Y = 256
GRID_X = 1024
N_GX = 8
N_GY = 4


def set_ends(values, rng, low, high):
    longest = values.shape.index(max(values.shape))
    spots = []
    for shift in (0, 1):
        where = [jax.random.randint(jax.random.fold_in(rng, axis), (), 0, length) for axis, length in enumerate(values.shape)]
        where[longest] = (where[longest] + shift) % values.shape[longest]
        spots.append(tuple(where))
    return values.at[spots[0]].set(low).at[spots[1]].set(high)


def levels(key, shape, pieces, low, high):
    gain = 1.0
    for position, parts in pieces:
        steps = jax.random.uniform(jax.random.fold_in(jax.random.fold_in(key, 6), position), (parts,), jnp.float32, low / len(pieces), high / len(pieces))
        gain = gain * jnp.repeat(jnp.exp(steps), shape[position] // parts).reshape((-1,) + (1,) * (len(shape) - 1 - position))
    return gain


def deal_out(rng, own, number, rows, number_of, top, reach, lean):
    ranking = jax.random.permutation(rng, number_of)
    packed, common = shares(number_of, rows * top, reach, lean, True), shares(number_of, rows * top, reach, lean, False)
    places = jnp.arange(number_of)

    def named(lengths, turn):
        used = int((lengths > 0).sum())
        fixed = max(1, used // 4)
        passed = fixed + (places - fixed + turn * (used - fixed)) % max(1, number_of - fixed)
        return jnp.zeros((number_of,), jnp.int32).at[ranking[jnp.where(places < fixed, places, passed)]].set(jnp.asarray(lengths, jnp.int32))

    lengths = jnp.where(number % 4 == 0, named(packed, number // 4), named(common, number - number // 4 - 1))
    mixed = jax.random.permutation(jax.random.fold_in(own, 3), number_of)
    donor, receiver = mixed[0:number_of // 2 * 2:2], mixed[1:number_of // 2 * 2:2]
    margin = jnp.minimum(lengths[donor] - 1, reach - lengths[receiver]) // 2
    margin = jnp.where((donor == ranking[0]) | (receiver == ranking[0]) | (lengths[receiver] == 0), 0, jnp.maximum(margin, 0))
    passed = jax.random.randint(jax.random.fold_in(own, 4), (number_of // 2,), 0, 1 << 20) % (margin + 1)
    lengths = lengths.at[donor].add(-passed).at[receiver].add(passed)
    labels = jnp.searchsorted(jnp.cumsum(lengths), jnp.arange(rows * top), side="right").astype(jnp.int32)
    listing = labels.reshape(top, rows).T
    listing = listing[jax.random.permutation(jax.random.fold_in(own, 1), rows)]
    turn = jax.random.randint(jax.random.fold_in(own, 2), (rows, 1), 0, top)
    return jnp.take_along_axis(listing, (jnp.arange(top)[None, :] + turn) % top, axis=1)


def shares(count, total, most, slope, full):
    portions = [(1 << 20) // math.isqrt(standing ** slope) + 1 for standing in range(1, count + 1)]
    largest = most if full else min(most, max(-(-total // count), total * portions[0] // sum(portions)))
    least = 1 if total - largest >= count - 1 else 0
    counts, surplus = [largest] + [least] * (count - 1), total - largest - least * (count - 1)
    while surplus > 0:
        movable = [i for i in range(1, count) if counts[i] < largest] or [i for i in range(1, count) if counts[i] < most]
        whole, budget = sum([portions[i] for i in movable]), surplus
        for i in movable:
            addition = min(most - counts[i], max(1, budget * portions[i] // whole), surplus)
            counts[i] = counts[i] + addition
            surplus = surplus - addition
    return np.array(counts)


def gaussian(stream_key, extent, width, reach, split=(), held_as=jnp.bfloat16):
    gain = levels(stream_key, extent, split, -0.22, 0.18) if split else 1.0
    array = jax.random.normal(stream_key, extent, jnp.float32) * width * gain
    return jnp.minimum(jnp.maximum(array, -reach), reach).astype(held_as)


def setup_inputs(seed: int = 0) -> dict:
    streams_of = jax.random.split(jax.random.key(seed), 10)
    ocean_fields = gaussian(streams_of[0], (OCEAN_TILES, FIELDS, TILE_CELLS), 1.0, 6.0, ((0, 32),))
    dest_device_keys = jax.random.split(jax.random.fold_in(streams_of[1], 1), OCEAN_TILES // OCEAN_DEV)
    dest_device_turns = jax.random.permutation(jax.random.fold_in(streams_of[1], 3), OCEAN_TILES // OCEAN_DEV)
    dest_device = jax.vmap(lambda own, number: deal_out(jax.random.fold_in(streams_of[1], 2), own, number, OCEAN_DEV, N_GX * N_GY, INTERSECTIONS, CAP, 2))(dest_device_keys, dest_device_turns).reshape((OCEAN_TILES, INTERSECTIONS))
    dest_tile = set_ends(jax.random.randint(streams_of[2], (OCEAN_TILES, INTERSECTIONS), 0, ATM_TILES), jax.random.fold_in(streams_of[2], 1), 0, ATM_TILES - 1).astype(jnp.int32)
    cell_target = set_ends(jax.random.randint(streams_of[3], (OCEAN_TILES, INTERSECTIONS, TILE_CELLS), 0, ATM_CELLS), jax.random.fold_in(streams_of[3], 1), 0, ATM_CELLS - 1).astype(jnp.int32)
    cell_weight = jnp.clip(jnp.exp(math.log(1.0) - 2.9996462 * jax.random.uniform(streams_of[4], (OCEAN_TILES, INTERSECTIONS, TILE_CELLS), jnp.float32) ** levels(streams_of[4], (OCEAN_TILES, INTERSECTIONS, TILE_CELLS), ((0, 32),), -0.2, 0.2)), 0.049804688, 1.0).astype(jnp.bfloat16)
    sea_mask = set_ends((jax.random.randint(streams_of[5], (OCEAN_TILES, TILE_CELLS), 0, 4) < 3).astype(jnp.int32), jax.random.fold_in(streams_of[5], 1), 0, 1)
    land_flux = gaussian(streams_of[6], (FIELDS, GRID_Y, GRID_X), 1.0, 6.0, ((1, 4), (2, 8)), jnp.float32)
    land_area = jnp.clip(jnp.exp(math.log(8.0) - 2.7725887 * jax.random.uniform(streams_of[7], (GRID_Y, GRID_X), jnp.float32) ** levels(streams_of[7], (GRID_Y, GRID_X), ((0, 4), (1, 8)), -0.2, 0.2)), 0.5, 8.0)
    kappa = jnp.clip(jnp.exp(math.log(0.24) - 2.4849066 * jax.random.uniform(streams_of[8], (GRID_Y, GRID_X), jnp.float32) ** levels(streams_of[8], (GRID_Y, GRID_X), ((0, 4), (1, 8)), -0.2, 0.2)), 0.02, 0.24)
    return dict(ocean_fields=ocean_fields, dest_device=dest_device, dest_tile=dest_tile, cell_target=cell_target, cell_weight=cell_weight, sea_mask=sea_mask, land_flux=land_flux, land_area=land_area, kappa=kappa)


def sweep_valid(padded, kpad):
    center = padded[:, 1:-1, 1:-1]
    kcenter = kpad[1:-1, 1:-1]
    result = center
    for near, knear in ((padded[:, 2:, 1:-1], kpad[2:, 1:-1]), (padded[:, :-2, 1:-1], kpad[:-2, 1:-1]), (padded[:, 1:-1, 2:], kpad[1:-1, 2:]), (padded[:, 1:-1, :-2], kpad[1:-1, :-2])):
        result = result + 0.5 * (kcenter + knear)[None] * (near - center)
    return result


def reference(ocean_fields, dest_device, dest_tile, cell_target, cell_weight, sea_mask, land_flux, land_area, kappa):
    weighted = cell_weight.astype(jnp.float32) * sea_mask[:, None, :].astype(jnp.float32)
    values = ocean_fields.astype(jnp.float32)[:, None, :, :] * weighted[:, :, None, :]
    col_dev = dest_device // N_GY
    row_dev = dest_device % N_GY
    rows = (row_dev * ATM_ROWS + dest_tile * TILE_ROWS)[:, :, None] + cell_target // ATM_COLS
    cols = (col_dev * ATM_COLS)[:, :, None] + cell_target % ATM_COLS
    flat_ids = (rows * GRID_X + cols).astype(jnp.int32).reshape(-1)
    numer = jax.ops.segment_sum(jnp.transpose(values, (0, 1, 3, 2)).reshape(-1, FIELDS), flat_ids, num_segments=GRID_Y * GRID_X)
    denom = jax.ops.segment_sum(weighted.reshape(-1), flat_ids, num_segments=GRID_Y * GRID_X)
    numer = numer.T.reshape(FIELDS, GRID_Y, GRID_X)
    denom = denom.reshape(GRID_Y, GRID_X)
    field = (numer + land_area[None] * land_flux) / (denom + land_area)[None]
    kpad = jnp.pad(kappa, 1)
    for sweep_index in range(SWEEPS):
        field = sweep_valid(jnp.pad(field, ((0, 0), (1, 1), (1, 1))), kpad)
    return field
```

```python
import functools

import jax
import jax.numpy as jnp
from jax import lax
from jax.experimental import pallas as pl
from jax.experimental.pallas import tpu as pltpu
from jax.sharding import PartitionSpec as P

TILE_ROWS = 8
ATM_COLS = 128
SWEEPS = 3
LAYERS = 4
EDGE = 4
LANE_BLOCK = 16

BF16 = jnp.bfloat16
F32 = jnp.float32
I32 = jnp.int32
VMEM = pl.BlockSpec(memory_space=pltpu.VMEM)
SMEM = pl.BlockSpec(memory_space=pltpu.SMEM)


def iota(shape, dim):
    return lax.broadcasted_iota(I32, shape, dim)


def params():
    return pltpu.CompilerParams(vmem_limit_bytes=40 << 20)


def pack_kernel(cap, group_s, group_v, fields, weights, codes, far_out, near_out, count):
    crossings, tiles = group_v.shape
    groups = 2 * far_out.shape[0]
    half = groups // 2
    slots = groups * cap

    hot = [
        (iota((groups, tiles), 0) == group_v[k : k + 1, :]).astype(F32) for k in range(crossings)
    ]
    before = (iota((tiles, tiles), 0) < iota((tiles, tiles), 1)).astype(BF16)
    offset = jnp.zeros((groups, 1), F32)
    packed_w = jnp.zeros((slots, weights.shape[2]), F32)
    packed_c = jnp.zeros((slots, weights.shape[2]), F32)
    for k in range(crossings):
        earlier = jnp.dot(hot[k].astype(BF16), before, preferred_element_type=F32) + offset
        offset = offset + jnp.sum(hot[k], axis=1, keepdims=True)
        within = jnp.sum(hot[k] * earlier, axis=0, keepdims=True).astype(I32)
        place = group_v[k : k + 1, :] * cap + within
        chosen = (iota((slots, tiles), 0) == place).astype(BF16)
        packed_w = packed_w + jnp.dot(chosen, weights[k], preferred_element_type=F32)
        packed_c = packed_c + jnp.dot(chosen, codes[k], preferred_element_type=F32)
    packed_w = packed_w.astype(BF16)
    packed_c = packed_c.astype(BF16)
    spare = jnp.zeros((8 - cap, weights.shape[2]), BF16)
    for g in range(groups):
        out, at = (far_out, g) if g < half else (near_out, g - half)
        for row, packed in ((cap, packed_w), (cap + 1, packed_c)):
            rows = packed[g * cap : (g + 1) * cap]
            out[at, row] = rows if cap == 8 else jnp.concatenate([rows, spare], axis=0)

    for g in range(groups):
        count[g] = 0

    for k in range(crossings):

        def place_pair(o, carry):
            g = group_s[k, o]
            n = count[g]
            count[g] = n + 1

            @pl.when(g < half)
            def _():
                far_out[g, n] = fields[o]

            @pl.when(g >= half)
            def _():
                near_out[g - half, n] = fields[o]

            return carry

        lax.fori_loop(0, tiles, place_pair, 0, unroll=4)

    empty = jnp.zeros(fields.shape[1:], BF16)
    for out, first in ((far_out, 0), (near_out, half)):

        def fill_group(g, carry):
            def fill(n, inner):
                out[g, n] = empty
                return inner

            return lax.fori_loop(count[first + g], cap, fill, carry)

        lax.fori_loop(0, half, fill_group, 0)


def pack(group, fields, weights, codes, cap, groups):
    shape = (groups // 2, cap + 2) + fields.shape[1:]
    return pl.pallas_call(
        functools.partial(pack_kernel, cap),
        out_shape=[jax.ShapeDtypeStruct(shape, BF16)] * 2,
        in_specs=[SMEM, VMEM, VMEM, VMEM, VMEM],
        out_specs=[VMEM, VMEM],
        scratch_shapes=[pltpu.SMEM((groups,), I32)],
        compiler_params=params(),
    )(group, group, fields, weights, codes)


def decode(code):
    tile = jnp.zeros(code.shape, I32)
    for k in range(1, 8):
        tile = tile + jnp.where(code >= 2.0 ** (7 + 8 * k), 1, 0)
    scaled = code
    for bit in (1, 2, 4):
        scaled = jnp.where((tile & bit) != 0, scaled * 2.0 ** (-8 * bit), scaled)
    cell = scaled.astype(I32)
    row = jnp.zeros(code.shape, I32)
    for k in range(1, 8):
        row = row + jnp.where(cell >= (1 << (7 + k)), 1, 0)
    return tile, row, lax.shift_right_logical(cell, row) - ATM_COLS


def bin_slots(cap, slots, total):
    sources, _, field_count, cells = slots.shape
    rows_here = total.shape[0] * TILE_ROWS // (TILE_ROWS + 1)
    zero = jnp.zeros((), BF16)
    total[...] = jnp.zeros_like(total)

    def source(g, carry):
        weight = slots[g, cap].astype(F32)
        tile, row, col = decode(slots[g, cap + 1].astype(F32))
        row16 = row.astype(F32).astype(BF16)
        col16 = col.astype(F32).astype(BF16)
        weight16 = weight.astype(BF16)
        for n in range(cap):
            field = slots[g, n]
            t = tile[n, 0]
            row_n = jnp.broadcast_to(row16[n : n + 1], (16, cells))
            twice = jnp.concatenate([field, field], axis=0)
            sub = iota((16, cells), 0)
            left = []
            for q in range(0, TILE_ROWS, 2):
                want = jnp.where(sub >= 8, q + 1.0, q + 0.0).astype(BF16)
                left.append(jnp.where(row_n == want, twice, zero))
            ones = jnp.ones((), BF16)
            left.append(jnp.where(row_n == sub.astype(F32).astype(BF16), ones, zero))
            right = jnp.where(
                jnp.broadcast_to(col16[n : n + 1], (ATM_COLS, cells))
                == iota((ATM_COLS, cells), 0).astype(F32).astype(BF16),
                jnp.broadcast_to(weight16[n : n + 1], (ATM_COLS, cells)),
                zero,
            )
            added = lax.dot_general(
                jnp.concatenate(left, axis=0),
                right,
                (((1,), (1,)), ((), ())),
                preferred_element_type=F32,
            )
            main = TILE_ROWS * field_count
            total[pl.ds(t * TILE_ROWS, TILE_ROWS)] += added[:main].reshape(
                TILE_ROWS, field_count, ATM_COLS
            )
            total[pl.ds(rows_here + t, 1)] += added[main : main + TILE_ROWS].reshape(
                1, TILE_ROWS, ATM_COLS
            )
        return carry

    lax.fori_loop(0, sources, source, 0, unroll=2)


def far_kernel(cap, slots, total):
    bin_slots(cap, slots, total)


def near_kernel(cap, slots, passed, land_flux, land_area, merged, strips, edges, total):
    bin_slots(cap, slots, total)
    field_count, rows_here, cols_here = land_flux.shape
    area = land_area[...]
    denom = (total[rows_here:] + passed[rows_here:]).reshape(rows_here, cols_here) + area
    lane = iota((rows_here, cols_here), 1)
    border = (lane < SWEEPS) | (lane >= cols_here - SWEEPS)
    numer = jnp.swapaxes(total[:rows_here] + passed[:rows_here], 0, 1)
    packed = jnp.zeros((rows_here, cols_here), F32)
    for f in range(field_count):
        value = (numer[f] + area * land_flux[f]) / denom
        merged[f] = value
        edges[f] = jnp.concatenate([value[:EDGE], value[rows_here - EDGE :]], axis=0)
        strip = jnp.where(border, value, 0.0)
        packed = packed + (pltpu.roll(strip, f * LANE_BLOCK, 1) if f else strip)
    strips[...] = packed


def cost(slots):
    sources, _, field_count, cells = slots.shape
    each = 2 * (field_count + 1) * TILE_ROWS * cells * ATM_COLS
    return pl.CostEstimate(
        flops=sources * 8 * each, bytes_accessed=slots.size * 2, transcendentals=0
    )


def bin_far(slots, cap, rows_here, field_count):
    shape = (rows_here // TILE_ROWS * (TILE_ROWS + 1), field_count, ATM_COLS)
    return pl.pallas_call(
        functools.partial(far_kernel, cap),
        out_shape=jax.ShapeDtypeStruct(shape, F32),
        in_specs=[VMEM],
        out_specs=VMEM,
        compiler_params=params(),
        cost_estimate=cost(slots),
    )(slots)


def bin_near(slots, passed, land_flux, land_area, cap):
    field_count, rows_here, cols_here = land_flux.shape
    return pl.pallas_call(
        functools.partial(near_kernel, cap),
        out_shape=[
            jax.ShapeDtypeStruct(land_flux.shape, F32),
            jax.ShapeDtypeStruct((rows_here, cols_here), F32),
            jax.ShapeDtypeStruct((field_count, 2 * EDGE, cols_here), F32),
        ],
        in_specs=[VMEM] * 4,
        out_specs=[VMEM] * 3,
        scratch_shapes=[pltpu.VMEM(passed.shape, F32)],
        compiler_params=params(),
        cost_estimate=cost(slots),
    )(slots, passed, land_flux, land_area)


def swaps(axis):
    count = lax.axis_size(axis)
    first = [(i, i ^ 1) for i in range(count) if i ^ 1 < count]
    second = [(i, i + 1) for i in range(1, count - 1, 2)]
    return first, second + [(b, a) for a, b in second]


def neighbours(values, axis):
    first, second = swaps(axis)
    one = lax.ppermute(values, axis, first)
    two = lax.ppermute(values, axis, second)
    odd = lax.axis_index(axis) % 2 == 1
    return jnp.where(odd, one, two), jnp.where(odd, two, one)


def select_columns(before, after, block):
    lane = iota(before.shape, 1) % block
    return jnp.where(lane < block // 2, after, before)


def ends(values):
    rows = values.shape[0]
    return jnp.concatenate([values[:EDGE], values[rows - EDGE :]], axis=0)


def coefficient_kernel(kappa, columns, above, below, out):
    padded = jnp.concatenate(
        [
            jnp.concatenate([kappa[...], below[0][:EDGE], above[0][EDGE:]], axis=0),
            jnp.concatenate([columns[...], below[1][:EDGE], above[1][EDGE:]], axis=0),
        ],
        axis=1,
    )
    lane = iota(padded.shape, 1)
    cols_here = kappa.shape[1]
    known = (lane < cols_here + SWEEPS) | (lane >= 2 * cols_here - SWEEPS)
    padded = jnp.where(known, padded, 0.0)
    inside = padded > 0.0
    for i, (shift, axis) in enumerate(NEIGHBOURS):
        near = pltpu.roll(padded, shift % padded.shape[axis], axis)
        out[i] = jnp.where(inside, 0.5 * (padded + near), 0.0)


NEIGHBOURS = ((-1, 0), (1, 0), (-1, 1), (1, 1))


def sweep_kernel(merged, before, after, above, below, coefficients, out):
    field_count, rows_here, cols_here = merged.shape
    lane = iota((rows_here, cols_here), 1)
    border = (lane < SWEEPS) | (lane >= cols_here - SWEEPS)
    columns = select_columns(before[...], after[...], LANE_BLOCK)
    lane8 = iota((2 * EDGE, cols_here), 1)
    border8 = (lane8 < SWEEPS) | (lane8 >= cols_here - SWEEPS)
    corner = jnp.concatenate([below[field_count][:EDGE], above[field_count][EDGE:]], axis=0)
    for f in range(field_count):
        shift = (cols_here - f * LANE_BLOCK) % cols_here
        side = pltpu.roll(columns, shift, 1) if f else columns
        far = pltpu.roll(corner, shift, 1) if f else corner
        rows = jnp.concatenate([below[f][:EDGE], above[f][EDGE:]], axis=0)
        u = jnp.concatenate(
            [
                jnp.concatenate([merged[f], rows], axis=0),
                jnp.concatenate(
                    [jnp.where(border, side, 0.0), jnp.where(border8, far, 0.0)], axis=0
                ),
            ],
            axis=1,
        )
        for _ in range(SWEEPS):
            new = u
            for i, (step, axis) in enumerate(NEIGHBOURS):
                near = pltpu.roll(u, step % u.shape[axis], axis)
                new = new + coefficients[i] * (near - u)
            u = new
        out[f] = u[:rows_here, :cols_here]


def shards(
    ocean_fields,
    dest_device,
    dest_tile,
    cell_target,
    cell_weight,
    sea_mask,
    land_flux,
    land_area,
    kappa,
):
    tiles_here, field_count, tile_cells = ocean_fields.shape
    crossing_count = dest_device.shape[1]
    width_x = lax.axis_size("gx")
    width_y = lax.axis_size("gy")
    device_count = width_x * width_y
    cap = max(2, tiles_here * crossing_count * 2 // device_count)
    half_x = width_x // 2
    layer_x = width_x // LAYERS
    rows_here, cols_here = land_area.shape

    owner = dest_device.T
    owner_x, owner_y = owner // width_y, owner % width_y
    mirror_x = (LAYERS - 1 - owner_x // layer_x) * layer_x + owner_x % layer_x
    near = owner_x // half_x == lax.axis_index("gx") // half_x
    stop_x = jnp.where(near, owner_x, mirror_x) % half_x
    group = stop_x * width_y + owner_y + jnp.where(near, device_count // 2, 0)

    weights = jnp.swapaxes(cell_weight * sea_mask[:, None, :].astype(BF16), 0, 1)
    scale = jnp.ones(dest_tile.shape, F32)
    for bit in (1, 2, 4):
        scale = scale * jnp.where((dest_tile & bit) != 0, 2.0 ** (8 * bit), 1.0)
    cell = (cell_target % ATM_COLS + ATM_COLS) << (cell_target // ATM_COLS)
    codes = jnp.swapaxes((cell.astype(F32) * scale[:, :, None]).astype(BF16), 0, 1)

    far_slots, near_slots = pack(group, ocean_fields, weights, codes, cap, device_count)
    halves = [
        [h * (device_count // 2) + i for i in range(device_count // 2)] for h in range(2)
    ]
    exchange = functools.partial(
        lax.all_to_all,
        axis_name=("gx", "gy"),
        split_axis=0,
        concat_axis=0,
        axis_index_groups=halves,
        tiled=True,
    )
    far_got = exchange(far_slots)
    near_got = exchange(near_slots)
    far_total = bin_far(far_got, cap, rows_here, field_count)
    mirror = [
        (i, (LAYERS - 1 - i // layer_x) * layer_x + i % layer_x) for i in range(width_x)
    ]
    passed = lax.ppermute(far_total, "gx", mirror)

    k_before, k_after = neighbours(kappa, "gx")
    k_columns = select_columns(k_before, k_after, cols_here)
    k_above, k_below = neighbours(jnp.stack([ends(kappa), ends(k_columns)]), "gy")
    coefficients = pl.pallas_call(
        coefficient_kernel,
        out_shape=jax.ShapeDtypeStruct((4, rows_here + 2 * EDGE, 2 * cols_here), F32),
        in_specs=[VMEM] * 4,
        out_specs=VMEM,
        compiler_params=params(),
    )(kappa, k_columns, k_above, k_below)

    merged, strips, edges = bin_near(near_got, passed, land_flux, land_area, cap)
    before, after = neighbours(strips, "gx")
    corners = ends(select_columns(before, after, LANE_BLOCK))
    above, below = neighbours(jnp.concatenate([edges, corners[None]], axis=0), "gy")
    return pl.pallas_call(
        sweep_kernel,
        out_shape=jax.ShapeDtypeStruct(merged.shape, F32),
        in_specs=[VMEM] * 6,
        out_specs=VMEM,
        compiler_params=params(),
    )(merged, before, after, above, below, coefficients)


def solution(mesh):
    return jax.shard_map(
        shards,
        mesh=mesh,
        in_specs=(
            P(("gx", "gy"), None, None),
            P(("gx", "gy"), None),
            P(("gx", "gy"), None),
            P(("gx", "gy"), None, None),
            P(("gx", "gy"), None, None),
            P(("gx", "gy"), None),
            P(None, "gy", "gx"),
            P("gy", "gx"),
            P("gy", "gx"),
        ),
        out_specs=P(None, "gy", "gx"),
        check_vma=False,
    )
```

```python
import functools

import jax
import jax.numpy as jnp
from jax import lax
from jax.experimental import pallas as pl
from jax.experimental.pallas import tpu as pltpu
from jax.sharding import PartitionSpec as P

TILE_ROWS = 8
ATM_COLS = 128
COL_BITS = 7
SWEEPS = 3
LAYERS = 4
EDGE = 4
LANE_BLOCK = 16

BF16 = jnp.bfloat16
F32 = jnp.float32
I32 = jnp.int32
VMEM = pl.BlockSpec(memory_space=pltpu.VMEM)
HBM = pl.BlockSpec(memory_space=pltpu.HBM)


def iota(shape, dim):
    return lax.broadcasted_iota(I32, shape, dim)


def params(megabytes=40):
    return pltpu.CompilerParams(vmem_limit_bytes=megabytes << 20)


def pack_kernel(
    cap,
    mirror,
    *refs,
):
    given, out, held, out_held = refs[:7], refs[7], refs[8:15], refs[15]
    count, source, in_sems, out_sems = refs[16:]
    copies = [
        pltpu.make_async_copy(given[i], held[i], in_sems.at[i]) for i in range(len(given))
    ]
    for copy in copies:
        copy.start()
    dest_s, dest_v, tile_v, target, weight, mask, fields = held
    crossings, tiles = dest_v.shape
    half, cells = out_held.shape[0], fields.shape[2]
    owners, slots = 2 * half, half * cap
    first = lax.axis_index("gx") // (lax.axis_size("gx") // 2) * half

    for d in range(owners):
        count[d] = 0

    def clear(i, carry):
        source[i] = 0
        return carry

    lax.fori_loop(0, owners * cap, clear, 0, unroll=16)
    copies[0].wait()
    for k in range(crossings):

        def enter(o, carry):
            d = dest_s[k, o]
            n = count[d]
            count[d] = n + 1
            source[d * cap + n] = o
            return carry

        lax.fori_loop(0, tiles, enter, 0, unroll=16)

    for copy in copies[1:6]:
        copy.wait()
    sea = mask[...] != 0
    every_weight = weight[...].astype(F32)
    before = (iota((tiles, tiles), 0) < iota((tiles, tiles), 1)).astype(BF16)
    offset = jnp.zeros((owners, 1), F32)
    packed_w = jnp.zeros((slots, cells), F32)
    packed_c = jnp.zeros((slots, cells), F32)
    for k in range(crossings):
        dest = dest_v[k : k + 1, :]
        hot = (iota((owners, tiles), 0) == dest).astype(F32)
        earlier = jnp.dot(hot.astype(BF16), before, preferred_element_type=F32) + offset
        offset = offset + jnp.sum(hot, axis=1, keepdims=True)
        within = jnp.sum(hot * earlier, axis=0, keepdims=True).astype(I32)
        place = ((dest ^ mirror) - first) * cap + within
        chosen = (iota((slots, tiles), 0) == place).astype(BF16)
        scale = jnp.ones(dest.shape, F32)
        for bit in (1, 2, 4):
            scale = scale * jnp.where((tile_v[k : k + 1, :] & bit) != 0, 2.0 ** (8 * bit), 1.0)
        cell = target[:, k, :]
        code = ((cell & (ATM_COLS - 1)) + ATM_COLS) << (cell >> COL_BITS)
        packed_w = packed_w + jnp.dot(
            chosen,
            jnp.where(sea, every_weight[:, k, :], 0.0).astype(BF16),
            preferred_element_type=F32,
        )
        packed_c = packed_c + jnp.dot(
            chosen * scale.astype(BF16), code.astype(F32).astype(BF16), preferred_element_type=F32
        )
    packed_w = packed_w.astype(BF16)
    packed_c = packed_c.astype(BF16)
    spare = jnp.zeros((8 - cap, cells), BF16)
    for g in range(half):
        for row, packed in ((cap, packed_w), (cap + 1, packed_c)):
            rows = packed[g * cap : (g + 1) * cap]
            out_held[g, row] = rows if cap == 8 else jnp.concatenate([rows, spare], axis=0)

    copies[6].wait()
    parts = out_sems.shape[0]
    step = half // parts
    sent = []
    for part in range(parts):

        def fill(g, carry):
            owner = (first + g) ^ mirror
            for n in range(cap):
                out_held[g, n] = fields[source[owner * cap + n]]
            return carry

        lax.fori_loop(part * step, (part + 1) * step, fill, 0, unroll=2)
        block = pl.ds(part * step, step)
        sent.append(pltpu.make_async_copy(out_held.at[block], out.at[block], out_sems.at[part]))
        sent[-1].start()
    for copy in sent:
        copy.wait()


def pack(dest, tile, target, weight, mask, fields, cap, owners, mirror):
    shape = (owners // 2, cap + 2) + fields.shape[1:]
    given = (dest, dest, tile, target, weight, mask, fields)
    return pl.pallas_call(
        functools.partial(pack_kernel, cap, mirror),
        out_shape=jax.ShapeDtypeStruct(shape, BF16),
        in_specs=[HBM] * len(given),
        out_specs=HBM,
        scratch_shapes=[pltpu.SMEM(dest.shape, I32)]
        + [pltpu.VMEM(a.shape, a.dtype) for a in given[1:]]
        + [
            pltpu.VMEM(shape, BF16),
            pltpu.SMEM((owners,), I32),
            pltpu.SMEM((owners * cap,), I32),
            pltpu.SemaphoreType.DMA((len(given),)),
            pltpu.SemaphoreType.DMA((4,)),
        ],
        compiler_params=params(62),
        cost_estimate=pl.CostEstimate(
            flops=10**8, bytes_accessed=4 * 10**6, transcendentals=0
        ),
    )(*given)


def decode(code):
    tile = jnp.zeros(code.shape, I32)
    for k in range(1, 8):
        tile = tile + jnp.where(code >= 2.0 ** (7 + 8 * k), 1, 0)
    scaled = code
    for bit in (1, 2, 4):
        scaled = jnp.where((tile & bit) != 0, scaled * 2.0 ** (-8 * bit), scaled)
    cell = scaled.astype(I32)
    row = jnp.zeros(code.shape, I32)
    for k in range(1, 8):
        row = row + jnp.where(cell >= (1 << (7 + k)), 1, 0)
    return tile, row, lax.shift_right_logical(cell, row) - ATM_COLS


def bin_slots(cap, slots, total):
    sources, _, field_count, cells = slots.shape
    rows_here = total.shape[0] * TILE_ROWS // (TILE_ROWS + 1)
    zero = jnp.zeros((), BF16)
    total[...] = jnp.zeros_like(total)

    def source(g, carry):
        weight = slots[g, cap].astype(F32)
        tile, row, col = decode(slots[g, cap + 1].astype(F32))
        row16 = row.astype(F32).astype(BF16)
        col16 = col.astype(F32).astype(BF16)
        weight16 = weight.astype(BF16)
        for n in range(cap):
            field = slots[g, n]
            t = tile[n, 0]
            row_n = jnp.broadcast_to(row16[n : n + 1], (16, cells))
            twice = jnp.concatenate([field, field], axis=0)
            sub = iota((16, cells), 0)
            left = []
            for q in range(0, TILE_ROWS, 2):
                want = jnp.where(sub >= 8, q + 1.0, q + 0.0).astype(BF16)
                left.append(jnp.where(row_n == want, twice, zero))
            ones = jnp.ones((), BF16)
            left.append(jnp.where(row_n == sub.astype(F32).astype(BF16), ones, zero))
            right = jnp.where(
                jnp.broadcast_to(col16[n : n + 1], (ATM_COLS, cells))
                == iota((ATM_COLS, cells), 0).astype(F32).astype(BF16),
                jnp.broadcast_to(weight16[n : n + 1], (ATM_COLS, cells)),
                zero,
            )
            added = lax.dot_general(
                jnp.concatenate(left, axis=0),
                right,
                (((1,), (1,)), ((), ())),
                preferred_element_type=F32,
            )
            main = TILE_ROWS * field_count
            total[pl.ds(t * TILE_ROWS, TILE_ROWS)] += added[:main].reshape(
                TILE_ROWS, field_count, ATM_COLS
            )
            total[pl.ds(rows_here + t, 1)] += added[main : main + TILE_ROWS].reshape(
                1, TILE_ROWS, ATM_COLS
            )
        return carry

    lax.fori_loop(0, sources, source, 0, unroll=2)


def merge_kernel(total, passed, land_flux, land_area, merged, strips, edges):
    field_count, rows_here, cols_here = land_flux.shape
    area = land_area[...]
    denom = (total[rows_here:] + passed[rows_here:]).reshape(rows_here, cols_here) + area
    lane = iota((rows_here, cols_here), 1)
    border = (lane < SWEEPS) | (lane >= cols_here - SWEEPS)
    numer = jnp.swapaxes(total[:rows_here] + passed[:rows_here], 0, 1)
    packed = jnp.zeros((rows_here, cols_here), F32)
    for f in range(field_count):
        value = (numer[f] + area * land_flux[f]) / denom
        merged[f] = value
        edges[f] = jnp.concatenate([value[:EDGE], value[rows_here - EDGE :]], axis=0)
        strip = jnp.where(border, value, 0.0)
        packed = packed + (pltpu.roll(strip, f * LANE_BLOCK, 1) if f else strip)
    strips[...] = packed


def cost(slots):
    sources, _, field_count, cells = slots.shape
    each = 2 * (field_count + 1) * TILE_ROWS * cells * ATM_COLS
    return pl.CostEstimate(
        flops=sources * 8 * each, bytes_accessed=slots.size * 2, transcendentals=0
    )


def bin_all(slots, cap, rows_here, field_count):
    shape = (rows_here // TILE_ROWS * (TILE_ROWS + 1), field_count, ATM_COLS)
    return pl.pallas_call(
        functools.partial(bin_slots, cap),
        out_shape=jax.ShapeDtypeStruct(shape, F32),
        in_specs=[VMEM],
        out_specs=VMEM,
        compiler_params=params(),
        cost_estimate=cost(slots),
    )(slots)


def merge(total, passed, land_flux, land_area):
    field_count, rows_here, cols_here = land_flux.shape
    return pl.pallas_call(
        merge_kernel,
        out_shape=[
            jax.ShapeDtypeStruct(land_flux.shape, F32),
            jax.ShapeDtypeStruct((rows_here, cols_here), F32),
            jax.ShapeDtypeStruct((field_count, 2 * EDGE, cols_here), F32),
        ],
        in_specs=[VMEM] * 4,
        out_specs=[VMEM] * 3,
        compiler_params=params(),
    )(total, passed, land_flux, land_area)


def swaps(axis):
    count = lax.axis_size(axis)
    first = [(i, i ^ 1) for i in range(count) if i ^ 1 < count]
    second = [(i, i + 1) for i in range(1, count - 1, 2)]
    return first, second + [(b, a) for a, b in second]


def neighbours(values, axis):
    first, second = swaps(axis)
    one = lax.ppermute(values, axis, first)
    two = lax.ppermute(values, axis, second)
    odd = lax.axis_index(axis) % 2 == 1
    return jnp.where(odd, one, two), jnp.where(odd, two, one)


def select_columns(before, after, block):
    lane = iota(before.shape, 1) % block
    return jnp.where(lane < block // 2, after, before)


def ends(values):
    rows = values.shape[0]
    return jnp.concatenate([values[:EDGE], values[rows - EDGE :]], axis=0)


NEIGHBOURS = ((-1, 0), (1, 0), (-1, 1), (1, 1))


def sweep_kernel(merged, before, after, above, below, kappa, k_columns, out):
    field_count, rows_here, cols_here = merged.shape

    def near(values, i):
        step, axis = NEIGHBOURS[i]
        return pltpu.roll(values, step % values.shape[axis], axis)

    def halo_rows(i):
        return jnp.concatenate([below[i][:EDGE], above[i][EDGE:]], axis=0)

    def whole(cells, rows, columns, corners):
        lane = iota((rows_here + 2 * EDGE, cols_here), 1)
        border = (lane < SWEEPS) | (lane >= cols_here - SWEEPS)
        side = jnp.concatenate([columns, corners], axis=0)
        return jnp.concatenate(
            [jnp.concatenate([cells, rows], axis=0), jnp.where(border, side, 0.0)], axis=1
        )

    k = whole(kappa[...], halo_rows(field_count + 1), k_columns[...], halo_rows(field_count + 2))
    coefficients = [
        jnp.where(k > 0.0, 0.5 * (k + near(k, i)), 0.0) for i in range(len(NEIGHBOURS))
    ]
    columns = select_columns(before[...], after[...], LANE_BLOCK)
    corners = halo_rows(field_count)
    for f in range(field_count):
        shift = (cols_here - f * LANE_BLOCK) % cols_here
        u = whole(
            merged[f],
            halo_rows(f),
            pltpu.roll(columns, shift, 1) if f else columns,
            pltpu.roll(corners, shift, 1) if f else corners,
        )
        for _ in range(SWEEPS):
            new = u
            for i, coefficient in enumerate(coefficients):
                new = new + coefficient * (near(u, i) - u)
            u = new
        out[f] = u[:rows_here, :cols_here]


def shards(
    ocean_fields,
    dest_device,
    dest_tile,
    cell_target,
    cell_weight,
    sea_mask,
    land_flux,
    land_area,
    kappa,
):
    tiles_here, field_count, tile_cells = ocean_fields.shape
    crossing_count = dest_device.shape[1]
    width_x = lax.axis_size("gx")
    width_y = lax.axis_size("gy")
    device_count = width_x * width_y
    cap = max(2, tiles_here * crossing_count * 2 // device_count)
    layer = width_x // LAYERS * width_y
    rows_here, cols_here = land_area.shape

    mirror = (LAYERS - 1) * layer
    pairs = (dest_device.T, dest_tile.T, cell_target, cell_weight, sea_mask, ocean_fields)
    halves = [
        [h * (device_count // 2) + i for i in range(device_count // 2)] for h in range(2)
    ]
    exchange = functools.partial(
        lax.all_to_all,
        axis_name=("gx", "gy"),
        split_axis=0,
        concat_axis=0,
        axis_index_groups=halves,
        tiled=True,
    )
    far_slots = pack(*pairs, cap, device_count, mirror)
    pairs, kappa, far_slots = lax.optimization_barrier((pairs, kappa, far_slots))
    far_got = exchange(far_slots)
    near_slots = pack(*pairs, cap, device_count, 0)
    k_columns = select_columns(*neighbours(kappa, "gx"), cols_here)
    near_slots, k_columns = lax.optimization_barrier((near_slots, k_columns))

    near_got = exchange(near_slots)
    far_total = bin_all(far_got, cap, rows_here, field_count)
    opposite = [(i, i ^ (mirror // width_y)) for i in range(width_x)]
    passed = lax.ppermute(far_total, "gx", opposite)
    total = bin_all(near_got, cap, rows_here, field_count)

    merged, strips, edges = merge(total, passed, land_flux, land_area)
    before, after = neighbours(strips, "gx")
    corners = ends(select_columns(before, after, LANE_BLOCK))
    rows = jnp.concatenate([edges, corners[None], ends(kappa)[None], ends(k_columns)[None]], axis=0)
    above, below = neighbours(rows, "gy")
    return pl.pallas_call(
        sweep_kernel,
        out_shape=jax.ShapeDtypeStruct(merged.shape, F32),
        in_specs=[VMEM] * 7,
        out_specs=VMEM,
        compiler_params=params(),
    )(merged, before, after, above, below, kappa, k_columns)


def solution(mesh):
    return jax.shard_map(
        shards,
        mesh=mesh,
        in_specs=(
            P(("gx", "gy"), None, None),
            P(("gx", "gy"), None),
            P(("gx", "gy"), None),
            P(("gx", "gy"), None, None),
            P(("gx", "gy"), None, None),
            P(("gx", "gy"), None),
            P(None, "gy", "gx"),
            P("gy", "gx"),
            P("gy", "gx"),
        ),
        out_specs=P(None, "gy", "gx"),
        check_vma=False,
    )
```

```python
import functools

import jax
import jax.numpy as jnp
from jax import lax
from jax.experimental import pallas as pl
from jax.experimental.pallas import tpu as pltpu
from jax.sharding import PartitionSpec as P

TILE_ROWS = 8
ATM_COLS = 128
COL_BITS = 7
SWEEPS = 3
LAYERS = 4
EDGE = 4
LANE_BLOCK = 14

BF16 = jnp.bfloat16
F32 = jnp.float32
I32 = jnp.int32
VMEM = pl.BlockSpec(memory_space=pltpu.VMEM)
HBM = pl.BlockSpec(memory_space=pltpu.HBM)
ANY = pl.BlockSpec(memory_space=pl.ANY)


def iota(shape, dim):
    return lax.broadcasted_iota(I32, shape, dim)


def params(megabytes=40):
    return pltpu.CompilerParams(vmem_limit_bytes=megabytes << 20)


def parity(number):
    for shift in (16, 8, 4, 2, 1):
        number = number ^ (number >> shift)
    return number & 1


def carried(position, core):
    return 2 * position + (parity(position) ^ 1 ^ core)


def pack_kernel(cap, near, mirror, *refs):
    given, outs, held, out_held = refs[:7], refs[7:-12], refs[-12:-5], refs[-5]
    count, source, in_sems, out_sems = refs[-4:]
    copies = [
        pltpu.make_async_copy(given[i], held[i], in_sems.at[i]) for i in range(len(given))
    ]
    for copy in copies:
        copy.start()
    dest_s, dest_v, tile_v, target, weight, mask, fields = held
    crossings, tiles = dest_v.shape
    half, cells = out_held.shape[0], fields.shape[2]
    owners, slots = 2 * half, half * cap
    me = lax.axis_index("gx") * lax.axis_size("gy") + lax.axis_index("gy")
    first = me // half * half
    here = me - first
    core = here & 1

    def block_of(owner):
        if not near:
            return (owner ^ mirror) - first
        index = owner - first
        distance = (index ^ here) >> 1
        carrier = 1 - parity(distance)
        block = (carrier ^ core) * (half // 2) + (distance >> 1) * 2 + ((index & 1) ^ carrier)
        return jnp.where((index >= 0) & (index < half), block, -1)

    def owner_of(block):
        if not near:
            return (first + block) ^ mirror
        carrier = core ^ (block // (half // 2))
        distance = carried((block % (half // 2)) >> 1, carrier)
        return first + (((here >> 1) ^ distance) << 1) + ((block & 1) ^ carrier)

    for d in range(owners):
        count[d] = 0

    def clear(i, carry):
        source[i] = 0
        return carry

    lax.fori_loop(0, owners * cap, clear, 0, unroll=16)
    copies[0].wait()
    for k in range(crossings):

        def enter(o, carry):
            d = dest_s[k, o]
            n = count[d]
            count[d] = n + 1
            source[d * cap + n] = o
            return carry

        lax.fori_loop(0, tiles, enter, 0, unroll=16)

    for copy in copies[1:6]:
        copy.wait()
    sea = mask[...] != 0
    every_weight = weight[...].astype(F32)
    before = (iota((tiles, tiles), 0) < iota((tiles, tiles), 1)).astype(BF16)
    offset = jnp.zeros((owners, 1), F32)
    packed_w = jnp.zeros((slots, cells), F32)
    packed_c = jnp.zeros((slots, cells), F32)
    for k in range(crossings):
        dest = dest_v[k : k + 1, :]
        hot = (iota((owners, tiles), 0) == dest).astype(F32)
        earlier = jnp.dot(hot.astype(BF16), before, preferred_element_type=F32) + offset
        offset = offset + jnp.sum(hot, axis=1, keepdims=True)
        within = jnp.sum(hot * earlier, axis=0, keepdims=True).astype(I32)
        chosen = (iota((slots, tiles), 0) == block_of(dest) * cap + within).astype(BF16)
        scale = jnp.ones(dest.shape, F32)
        for bit in (1, 2, 4):
            scale = scale * jnp.where((tile_v[k : k + 1, :] & bit) != 0, 2.0 ** (8 * bit), 1.0)
        cell = target[:, k, :]
        code = ((cell & (ATM_COLS - 1)) + ATM_COLS) << (cell >> COL_BITS)
        packed_w = packed_w + jnp.dot(
            chosen,
            jnp.where(sea, every_weight[:, k, :], 0.0).astype(BF16),
            preferred_element_type=F32,
        )
        packed_c = packed_c + jnp.dot(
            chosen * scale.astype(BF16), code.astype(F32).astype(BF16), preferred_element_type=F32
        )
    packed_w = packed_w.astype(BF16)
    packed_c = packed_c.astype(BF16)
    spare = jnp.zeros((8 - cap, cells), BF16)
    for g in range(half):
        for row, packed in ((cap, packed_w), (cap + 1, packed_c)):
            rows = packed[g * cap : (g + 1) * cap]
            out_held[g, row] = rows if cap == 8 else jnp.concatenate([rows, spare], axis=0)

    copies[6].wait()
    step = half // out_sems.shape[0]
    sent = []
    for part in range(out_sems.shape[0]):

        def fill(g, carry):
            owner = owner_of(g)
            for n in range(cap):
                out_held[g, n] = fields[source[owner * cap + n]]
            return carry

        lax.fori_loop(part * step, (part + 1) * step, fill, 0, unroll=2)
        block = pl.ds(part * step, step)
        out = outs[part * step // outs[0].shape[0]]
        into = out.at[pl.ds(part * step % out.shape[0], step)]
        sent.append(pltpu.make_async_copy(out_held.at[block], into, out_sems.at[part]))
        sent[-1].start()
    for copy in sent:
        copy.wait()


def pack(dest, tile, target, weight, mask, fields, cap, owners, near, mirror):
    half = owners // 2
    shape = (half, cap + 2) + fields.shape[1:]
    parts = 2 if near else 1
    given = (dest, dest, tile, target, weight, mask, fields)
    return pl.pallas_call(
        functools.partial(pack_kernel, cap, near, mirror),
        out_shape=[jax.ShapeDtypeStruct((half // parts,) + shape[1:], BF16)] * parts,
        in_specs=[HBM] * len(given),
        out_specs=[HBM] * parts,
        scratch_shapes=[pltpu.SMEM(dest.shape, I32)]
        + [pltpu.VMEM(a.shape, a.dtype) for a in given[1:]]
        + [
            pltpu.VMEM(shape, BF16),
            pltpu.SMEM((owners,), I32),
            pltpu.SMEM((owners * cap,), I32),
            pltpu.SemaphoreType.DMA((len(given),)),
            pltpu.SemaphoreType.DMA((4,)),
        ],
        compiler_params=params(62),
        cost_estimate=pl.CostEstimate(
            flops=10**8, bytes_accessed=4 * 10**6, transcendentals=0
        ),
    )(*given)


def join_kernel(kept, taken, *refs):
    outs, (held, in_sems, out_sems) = refs[:-3], refs[-3:]
    arriving = []
    for j in range(len(outs)):
        for rel in range(2):
            for src, blocks in enumerate((kept, taken)):
                at = 4 * j + 2 * rel + src
                copy = pltpu.make_async_copy(blocks.at[2 * j + rel], held.at[at], in_sems.at[at])
                copy.start()
                arriving.append(copy)
    leaving = []
    for j, out in enumerate(outs):
        for copy in arriving[4 * j : 4 * j + 4]:
            copy.wait()
        leaving.append(pltpu.make_async_copy(held.at[pl.ds(4 * j, 4)], out, out_sems.at[j]))
        leaving[-1].start()
    for copy in leaving:
        copy.wait()


def join(kept, taken):
    number = taken.shape[0] // 2
    return pl.pallas_call(
        join_kernel,
        out_shape=[jax.ShapeDtypeStruct((4,) + taken.shape[1:], BF16)] * number,
        in_specs=[HBM] * 2,
        out_specs=[HBM] * number,
        scratch_shapes=[
            pltpu.VMEM((4 * number,) + taken.shape[1:], BF16),
            pltpu.SemaphoreType.DMA((4 * number,)),
            pltpu.SemaphoreType.DMA((number,)),
        ],
        compiler_params=params(62),
        cost_estimate=pl.CostEstimate(
            flops=0, bytes_accessed=4 * taken.size * 2, transcendentals=0
        ),
    )(kept, taken)


def decode(code):
    tile = jnp.zeros(code.shape, I32)
    for k in range(1, 8):
        tile = tile + jnp.where(code >= 2.0 ** (7 + 8 * k), 1, 0)
    scaled = code
    for bit in (1, 2, 4):
        scaled = jnp.where((tile & bit) != 0, scaled * 2.0 ** (-8 * bit), scaled)
    cell = scaled.astype(I32)
    row = jnp.zeros(code.shape, I32)
    for k in range(1, 8):
        row = row + jnp.where(cell >= (1 << (7 + k)), 1, 0)
    return tile, row, lax.shift_right_logical(cell, row) - ATM_COLS


def bin_slots(cap, picked, earlier, *refs):
    arrays = len(refs) - 2 - (2 if earlier else 1) * len(picked)
    given, refs = refs[:arrays], refs[arrays:]
    before = refs[: len(picked)] if earlier else ()
    totals = refs[len(before) : len(before) + len(picked)]
    slots, sems = refs[-2:]
    copies, bounds = [], []
    for pick in picked:
        low = sum(copy[2] for copy in copies)
        for array, first, number in pick:
            at = sum(copy[2] for copy in copies)
            copies.append((array, first, number, at))
        bounds.append((low, sum(copy[2] for copy in copies)))
    started = []
    for i, (array, first, number, at) in enumerate(copies):
        copy = pltpu.make_async_copy(
            given[array].at[pl.ds(first, number)], slots.at[pl.ds(at, number)], sems.at[i]
        )
        copy.start()
        started.append(copy)
    for i, total in enumerate(totals):
        total[...] = before[i][...] if earlier else jnp.zeros_like(total)
    for copy in started:
        copy.wait()
    for total, (low, high) in zip(totals, bounds, strict=True):
        bin_range(cap, slots, low, high, total)


def bin_range(cap, slots, low, high, total):
    sources, _, field_count, cells = slots.shape
    rows_here = total.shape[0] * TILE_ROWS // (TILE_ROWS + 1)
    zero = jnp.zeros((), BF16)

    def source(g, carry):
        weight = slots[g, cap].astype(F32)
        tile, row, col = decode(slots[g, cap + 1].astype(F32))
        row16 = row.astype(F32).astype(BF16)
        col16 = col.astype(F32).astype(BF16)
        weight16 = weight.astype(BF16)
        for n in range(cap):
            field = slots[g, n]
            t = tile[n, 0]
            row_n = jnp.broadcast_to(row16[n : n + 1], (16, cells))
            twice = jnp.concatenate([field, field], axis=0)
            sub = iota((16, cells), 0)
            left = []
            for q in range(0, TILE_ROWS, 2):
                want = jnp.where(sub >= 8, q + 1.0, q + 0.0).astype(BF16)
                left.append(jnp.where(row_n == want, twice, zero))
            ones = jnp.ones((), BF16)
            left.append(jnp.where(row_n == sub.astype(F32).astype(BF16), ones, zero))
            right = jnp.where(
                jnp.broadcast_to(col16[n : n + 1], (ATM_COLS, cells))
                == iota((ATM_COLS, cells), 0).astype(F32).astype(BF16),
                jnp.broadcast_to(weight16[n : n + 1], (ATM_COLS, cells)),
                zero,
            )
            added = lax.dot_general(
                jnp.concatenate(left, axis=0),
                right,
                (((1,), (1,)), ((), ())),
                preferred_element_type=F32,
            )
            main = TILE_ROWS * field_count
            total[pl.ds(t * TILE_ROWS, TILE_ROWS)] += added[:main].reshape(
                TILE_ROWS, field_count, ATM_COLS
            )
            total[pl.ds(rows_here + t, 1)] += added[main : main + TILE_ROWS].reshape(
                1, TILE_ROWS, ATM_COLS
            )
        return carry

    lax.fori_loop(low, high, source, 0, unroll=2 if (high - low) % 2 == 0 else 1)


def merge_kernel(total, other, passed, land_flux, land_area, kappa, merged, strips, edges):
    field_count, rows_here, cols_here = land_flux.shape
    area = land_area[...]
    denom = total[rows_here:] + other[rows_here:] + passed[rows_here:]
    denom = denom.reshape(rows_here, cols_here) + area
    lane = iota((rows_here, cols_here), 1)
    border = (lane < SWEEPS) | (lane >= cols_here - SWEEPS)
    numer = total[:rows_here] + other[:rows_here] + passed[:rows_here]
    numer = jnp.swapaxes(numer, 0, 1)
    packed = jnp.zeros((rows_here, cols_here), F32)
    for f in range(field_count + 1):
        if f < field_count:
            value = (numer[f] + area * land_flux[f]) / denom
            merged[f] = value
        else:
            value = kappa[...]
        edges[f] = jnp.concatenate([value[:EDGE], value[rows_here - EDGE :]], axis=0)
        strip = jnp.where(border, value, 0.0)
        packed = packed + (pltpu.roll(strip, f * LANE_BLOCK, 1) if f else strip)
    strips[...] = packed


def bin_all(arrays, picked, earlier, cap, rows_here):
    _, rows, field_count, cells = arrays[0].shape
    shape = (rows_here // TILE_ROWS * (TILE_ROWS + 1), field_count, ATM_COLS)
    number = sum(part[2] for pick in picked for part in pick)
    each = 2 * (field_count + 1) * TILE_ROWS * cells * ATM_COLS
    return pl.pallas_call(
        functools.partial(bin_slots, cap, picked, bool(earlier)),
        out_shape=[jax.ShapeDtypeStruct(shape, F32)] * len(picked),
        in_specs=[ANY] * len(arrays) + [VMEM] * len(earlier),
        out_specs=[VMEM] * len(picked),
        scratch_shapes=[
            pltpu.VMEM((number,) + arrays[0].shape[1:], BF16),
            pltpu.SemaphoreType.DMA((sum(len(pick) for pick in picked),)),
        ],
        compiler_params=params(),
        cost_estimate=pl.CostEstimate(
            flops=number * 8 * each,
            bytes_accessed=number * rows * field_count * cells * 2,
            transcendentals=0,
        ),
    )(*arrays, *earlier)


def merge(total, other, passed, land_flux, land_area, kappa):
    field_count, rows_here, cols_here = land_flux.shape
    return pl.pallas_call(
        merge_kernel,
        out_shape=[
            jax.ShapeDtypeStruct(land_flux.shape, F32),
            jax.ShapeDtypeStruct((rows_here, cols_here), F32),
            jax.ShapeDtypeStruct((field_count + 1, 2 * EDGE, cols_here), F32),
        ],
        in_specs=[VMEM] * 6,
        out_specs=[VMEM] * 3,
        compiler_params=params(),
    )(total, other, passed, land_flux, land_area, kappa)


def swaps(axis):
    count = lax.axis_size(axis)
    first = [(i, i ^ 1) for i in range(count) if i ^ 1 < count]
    second = [(i, i + 1) for i in range(1, count - 1, 2)]
    return first, second + [(b, a) for a, b in second]


def neighbours(values, axis):
    first, second = swaps(axis)
    one = lax.ppermute(values, axis, first)
    two = lax.ppermute(values, axis, second)
    odd = lax.axis_index(axis) % 2 == 1
    return jnp.where(odd, one, two), jnp.where(odd, two, one)


def select_columns(before, after):
    lane = (iota(before.shape, 1) + SWEEPS) % before.shape[1] % LANE_BLOCK
    return jnp.where(lane < SWEEPS, before, after)


def ends(values):
    rows = values.shape[0]
    return jnp.concatenate([values[:EDGE], values[rows - EDGE :]], axis=0)


NEIGHBOURS = ((-1, 0), (1, 0), (-1, 1), (1, 1))


def sweep_kernel(merged, before, after, above, below, kappa, out):
    field_count, rows_here, cols_here = merged.shape

    def near(values, i):
        step, axis = NEIGHBOURS[i]
        return pltpu.roll(values, step % values.shape[axis], axis)

    def halo_rows(i):
        return jnp.concatenate([below[i][:EDGE], above[i][EDGE:]], axis=0)

    columns = select_columns(before[...], after[...])
    corners = halo_rows(field_count + 1)
    lane = iota((rows_here + 2 * EDGE, cols_here), 1)
    border = (lane < SWEEPS) | (lane >= cols_here - SWEEPS)

    def whole(cells, f):
        side = jnp.concatenate([columns, corners], axis=0)
        side = pltpu.roll(side, (cols_here - f * LANE_BLOCK) % cols_here, 1) if f else side
        return jnp.concatenate(
            [jnp.concatenate([cells, halo_rows(f)], axis=0), jnp.where(border, side, 0.0)], axis=1
        )

    k = whole(kappa[...], field_count)
    coefficients = [
        jnp.where(k > 0.0, 0.5 * (k + near(k, i)), 0.0) for i in range(len(NEIGHBOURS))
    ]
    for f in range(field_count):
        u = whole(merged[f], f)
        for _ in range(SWEEPS):
            new = u
            for i, coefficient in enumerate(coefficients):
                new = new + coefficient * (near(u, i) - u)
            u = new
        out[f] = u[:rows_here, :cols_here]


def shards(
    ocean_fields,
    dest_device,
    dest_tile,
    cell_target,
    cell_weight,
    sea_mask,
    land_flux,
    land_area,
    kappa,
):
    tiles_here, field_count, tile_cells = ocean_fields.shape
    crossing_count = dest_device.shape[1]
    width_x = lax.axis_size("gx")
    width_y = lax.axis_size("gy")
    device_count = width_x * width_y
    cap = max(2, tiles_here * crossing_count * 2 // device_count)
    layer = width_x // LAYERS * width_y
    rows_here, cols_here = land_area.shape

    mirror = (LAYERS - 1) * layer
    pairs = (dest_device.T, dest_tile.T, cell_target, cell_weight, sea_mask, ocean_fields)
    halves = [
        [h * (device_count // 2) + i for i in range(device_count // 2)] for h in range(2)
    ]
    exchange = functools.partial(
        lax.all_to_all,
        axis_name=("gx", "gy"),
        split_axis=0,
        concat_axis=0,
        axis_index_groups=halves,
        tiled=True,
    )
    half = device_count // 2
    everywhere = range(device_count)
    far_slots = pack(*pairs, cap, device_count, False, mirror)[0]
    pairs, far_slots = lax.optimization_barrier((pairs, far_slots))
    far_got = exchange(far_slots)
    kept, given = pack(*pairs, cap, device_count, True, 0)
    taken = lax.ppermute(given, ("gx", "gy"), [(i, i ^ 1) for i in everywhere])
    got = [
        lax.ppermute(message, ("gx", "gy"), [(i, i ^ 2 * carried(j, i & 1)) for i in everywhere])
        for j, message in enumerate(join(kept, taken))
    ]

    far_total = bin_all([far_got], [[(0, 0, half)]], [], cap, rows_here)[0]
    opposite = [(i, i ^ (mirror // width_y)) for i in range(width_x)]
    passed = lax.ppermute(far_total, "gx", opposite)
    got, far_total = lax.optimization_barrier((got, far_total))
    other = bin_all(got, [[(j, 2, 2) for j in range(len(got))]], [], cap, rows_here)[0]
    other = lax.ppermute(other, ("gx", "gy"), [(i, i ^ 1) for i in everywhere])
    total = bin_all(got, [[(j, 0, 2) for j in range(len(got))]], [], cap, rows_here)[0]

    merged, strips, edges = merge(total, other, passed, land_flux, land_area, kappa)
    before, after = neighbours(strips, "gx")
    corners = ends(select_columns(before, after))
    above, below = neighbours(jnp.concatenate([edges, corners[None]], axis=0), "gy")
    return pl.pallas_call(
        sweep_kernel,
        out_shape=jax.ShapeDtypeStruct(merged.shape, F32),
        in_specs=[VMEM] * 6,
        out_specs=VMEM,
        compiler_params=params(),
    )(merged, before, after, above, below, kappa)


def solution(mesh):
    return jax.shard_map(
        shards,
        mesh=mesh,
        in_specs=(
            P(("gx", "gy"), None, None),
            P(("gx", "gy"), None),
            P(("gx", "gy"), None),
            P(("gx", "gy"), None, None),
            P(("gx", "gy"), None, None),
            P(("gx", "gy"), None),
            P(None, "gy", "gx"),
            P("gy", "gx"),
            P("gy", "gx"),
        ),
        out_specs=P(None, "gy", "gx"),
        check_vma=False,
    )
```

```python
import functools

import jax
import jax.numpy as jnp
from jax import lax
from jax.experimental import pallas as pl
from jax.experimental.pallas import tpu as pltpu
from jax.sharding import PartitionSpec as P

TILE_ROWS = 8
ATM_COLS = 128
COL_BITS = 7
SWEEPS = 3
LAYERS = 4
EDGE = 4
TOGETHER = 8
LANE_BLOCK = 14

BF16 = jnp.bfloat16
F32 = jnp.float32
I32 = jnp.int32
VMEM = pl.BlockSpec(memory_space=pltpu.VMEM)
HBM = pl.BlockSpec(memory_space=pltpu.HBM)
ANY = pl.BlockSpec(memory_space=pl.ANY)


def iota(shape, dim):
    return lax.broadcasted_iota(I32, shape, dim)


def params(megabytes=40):
    return pltpu.CompilerParams(vmem_limit_bytes=megabytes << 20)


def parity(number):
    for shift in (16, 8, 4, 2, 1):
        number = number ^ (number >> shift)
    return number & 1


def carried(position, core):
    return 2 * position + (parity(position) ^ 1 ^ core)


def pack_kernel(cap, near, mirror, *refs):
    given, outs, held, out_held = refs[:7], refs[7:-12], refs[-12:-5], refs[-5]
    count, source, in_sems, out_sems = refs[-4:]
    copies = [
        pltpu.make_async_copy(given[i], held[i], in_sems.at[i]) for i in range(len(given))
    ]
    for copy in copies:
        copy.start()
    dest_s, dest_v, tile_v, target, weight, mask, fields = held
    crossings, tiles = dest_v.shape
    half, cells = out_held.shape[0], fields.shape[2]
    owners, slots = 2 * half, half * cap
    me = lax.axis_index("gx") * lax.axis_size("gy") + lax.axis_index("gy")
    first = me // half * half
    here = me - first
    core = here & 1

    def block_of(owner):
        if not near:
            return (owner ^ mirror) - first
        index = owner - first
        distance = (index ^ here) >> 1
        carrier = 1 - parity(distance)
        block = (carrier ^ core) * (half // 2) + (distance >> 1) * 2 + ((index & 1) ^ carrier)
        return jnp.where((index >= 0) & (index < half), block, -1)

    def owner_of(block):
        if not near:
            return (first + block) ^ mirror
        carrier = core ^ (block // (half // 2))
        distance = carried((block % (half // 2)) >> 1, carrier)
        return first + (((here >> 1) ^ distance) << 1) + ((block & 1) ^ carrier)

    for d in range(owners):
        count[d] = 0

    def clear(i, carry):
        source[i] = 0
        return carry

    lax.fori_loop(0, owners * cap, clear, 0, unroll=16)
    copies[0].wait()
    for k in range(crossings):

        def enter(o, carry):
            d = dest_s[k, o]
            n = count[d]
            count[d] = n + 1
            source[d * cap + n] = o
            return carry

        lax.fori_loop(0, tiles, enter, 0, unroll=16)

    for copy in copies[1:6]:
        copy.wait()
    sea = mask[...] != 0
    every_weight = weight[...].astype(F32)
    before = (iota((tiles, tiles), 0) < iota((tiles, tiles), 1)).astype(BF16)
    offset = jnp.zeros((owners, 1), F32)
    packed_w = jnp.zeros((slots, cells), F32)
    packed_c = jnp.zeros((slots, cells), F32)
    for k in range(crossings):
        dest = dest_v[k : k + 1, :]
        hot = (iota((owners, tiles), 0) == dest).astype(F32)
        earlier = jnp.dot(hot.astype(BF16), before, preferred_element_type=F32) + offset
        offset = offset + jnp.sum(hot, axis=1, keepdims=True)
        within = jnp.sum(hot * earlier, axis=0, keepdims=True).astype(I32)
        chosen = (iota((slots, tiles), 0) == block_of(dest) * cap + within).astype(BF16)
        scale = jnp.ones(dest.shape, F32)
        for bit in (1, 2, 4):
            scale = scale * jnp.where((tile_v[k : k + 1, :] & bit) != 0, 2.0 ** (8 * bit), 1.0)
        cell = target[:, k, :]
        code = ((cell & (ATM_COLS - 1)) + ATM_COLS) << (cell >> COL_BITS)
        packed_w = packed_w + jnp.dot(
            chosen,
            jnp.where(sea, every_weight[:, k, :], 0.0).astype(BF16),
            preferred_element_type=F32,
        )
        packed_c = packed_c + jnp.dot(
            chosen * scale.astype(BF16), code.astype(F32).astype(BF16), preferred_element_type=F32
        )
    packed_w = packed_w.astype(BF16)
    packed_c = packed_c.astype(BF16)
    spare = jnp.zeros((8 - cap, cells), BF16)
    for g in range(half):
        for row, packed in ((cap, packed_w), (cap + 1, packed_c)):
            rows = packed[g * cap : (g + 1) * cap]
            out_held[g, row] = rows if cap == 8 else jnp.concatenate([rows, spare], axis=0)

    copies[6].wait()
    step = half // out_sems.shape[0]
    sent = []
    for part in range(out_sems.shape[0]):

        def fill(g, carry):
            owner = owner_of(g)
            for n in range(cap):
                out_held[g, n] = fields[source[owner * cap + n]]
            return carry

        lax.fori_loop(part * step, (part + 1) * step, fill, 0, unroll=2)
        block = pl.ds(part * step, step)
        out = outs[part * step // outs[0].shape[0]]
        into = out.at[pl.ds(part * step % out.shape[0], step)]
        sent.append(pltpu.make_async_copy(out_held.at[block], into, out_sems.at[part]))
        sent[-1].start()
    for copy in sent:
        copy.wait()


def pack(dest, tile, target, weight, mask, fields, cap, owners, near, mirror):
    half = owners // 2
    shape = (half, cap + 2) + fields.shape[1:]
    parts = 2 if near else 1
    given = (dest, dest, tile, target, weight, mask, fields)
    return pl.pallas_call(
        functools.partial(pack_kernel, cap, near, mirror),
        out_shape=[jax.ShapeDtypeStruct((half // parts,) + shape[1:], BF16)] * parts,
        in_specs=[HBM] * len(given),
        out_specs=[HBM] * parts,
        scratch_shapes=[pltpu.SMEM(dest.shape, I32)]
        + [pltpu.VMEM(a.shape, a.dtype) for a in given[1:]]
        + [
            pltpu.VMEM(shape, BF16),
            pltpu.SMEM((owners,), I32),
            pltpu.SMEM((owners * cap,), I32),
            pltpu.SemaphoreType.DMA((len(given),)),
            pltpu.SemaphoreType.DMA((4,)),
        ],
        compiler_params=params(62),
        cost_estimate=pl.CostEstimate(
            flops=10**8, bytes_accessed=4 * 10**6, transcendentals=0
        ),
    )(*given)


def join_kernel(kept, taken, *refs):
    outs, (held, in_sems, out_sems) = refs[:-3], refs[-3:]
    arriving = []
    for j in range(len(outs)):
        for rel in range(2):
            for src, blocks in enumerate((kept, taken)):
                at = 4 * j + 2 * rel + src
                copy = pltpu.make_async_copy(blocks.at[2 * j + rel], held.at[at], in_sems.at[at])
                copy.start()
                arriving.append(copy)
    leaving = []
    for j, out in enumerate(outs):
        for copy in arriving[4 * j : 4 * j + 4]:
            copy.wait()
        leaving.append(pltpu.make_async_copy(held.at[pl.ds(4 * j, 4)], out, out_sems.at[j]))
        leaving[-1].start()
    for copy in leaving:
        copy.wait()


def join(kept, taken):
    number = taken.shape[0] // 2
    return pl.pallas_call(
        join_kernel,
        out_shape=[jax.ShapeDtypeStruct((4,) + taken.shape[1:], BF16)] * number,
        in_specs=[HBM] * 2,
        out_specs=[HBM] * number,
        scratch_shapes=[
            pltpu.VMEM((4 * number,) + taken.shape[1:], BF16),
            pltpu.SemaphoreType.DMA((4 * number,)),
            pltpu.SemaphoreType.DMA((number,)),
        ],
        compiler_params=params(62),
        cost_estimate=pl.CostEstimate(
            flops=0, bytes_accessed=4 * taken.size * 2, transcendentals=0
        ),
    )(kept, taken)


def decode(code):
    tile = jnp.zeros(code.shape, I32)
    for k in range(1, 8):
        tile = tile + jnp.where(code >= 2.0 ** (7 + 8 * k), 1, 0)
    scaled = code
    for bit in (1, 2, 4):
        scaled = jnp.where((tile & bit) != 0, scaled * 2.0 ** (-8 * bit), scaled)
    cell = scaled.astype(I32)
    row = jnp.zeros(code.shape, I32)
    for k in range(1, 8):
        row = row + jnp.where(cell >= (1 << (7 + k)), 1, 0)
    return tile, row, lax.shift_right_logical(cell, row) - ATM_COLS


def bin_slots(cap, picked, arrays, *refs):
    given, before, totals = refs[:arrays], refs[arrays : -len(picked)], refs[-len(picked) :]
    for n, (pick, total) in enumerate(zip(picked, totals, strict=True)):
        total[...] = before[n][...] if before else jnp.zeros_like(total)
        for array, first, number in pick:
            together = min(number, TOGETHER)

            def some(i, carry):
                for block in range(together):
                    bin_block(cap, given[array], first + i * together + block, total)
                return carry

            lax.fori_loop(0, number // together, some, 0, unroll=number == together)


def bin_block(cap, slots, i, total):
    field_count, cells = slots.shape[2:]
    rows_here = total.shape[0] * TILE_ROWS // (TILE_ROWS + 1)
    zero = jnp.zeros((), BF16)
    weight = slots[i, cap].astype(F32)
    tile, row, col = decode(slots[i, cap + 1].astype(F32))
    row16 = row.astype(F32).astype(BF16)
    col16 = col.astype(F32).astype(BF16)
    weight16 = weight.astype(BF16)
    for n in range(cap):
        field = slots[i, n]
        t = tile[n, 0]
        row_n = jnp.broadcast_to(row16[n : n + 1], (16, cells))
        twice = jnp.concatenate([field, field], axis=0)
        sub = iota((16, cells), 0)
        left = []
        for q in range(0, TILE_ROWS, 2):
            want = jnp.where(sub >= 8, q + 1.0, q + 0.0).astype(BF16)
            left.append(jnp.where(row_n == want, twice, zero))
        ones = jnp.ones((), BF16)
        left.append(jnp.where(row_n == sub.astype(F32).astype(BF16), ones, zero))
        right = jnp.where(
            jnp.broadcast_to(col16[n : n + 1], (ATM_COLS, cells))
            == iota((ATM_COLS, cells), 0).astype(F32).astype(BF16),
            jnp.broadcast_to(weight16[n : n + 1], (ATM_COLS, cells)),
            zero,
        )
        added = lax.dot_general(
            jnp.concatenate(left, axis=0),
            right,
            (((1,), (1,)), ((), ())),
            preferred_element_type=F32,
        )
        main = TILE_ROWS * field_count
        total[pl.ds(t * TILE_ROWS, TILE_ROWS)] += added[:main].reshape(
            TILE_ROWS, field_count, ATM_COLS
        )
        total[pl.ds(rows_here + t, 1)] += added[main : main + TILE_ROWS].reshape(
            1, TILE_ROWS, ATM_COLS
        )


def merge_kernel(total, other, passed, land_flux, land_area, kappa, merged, strips, edges):
    field_count, rows_here, cols_here = land_flux.shape
    area = land_area[...]
    denom = total[rows_here:] + other[rows_here:] + passed[rows_here:]
    denom = denom.reshape(rows_here, cols_here) + area
    lane = iota((rows_here, cols_here), 1)
    border = (lane < SWEEPS) | (lane >= cols_here - SWEEPS)
    numer = total[:rows_here] + other[:rows_here] + passed[:rows_here]
    numer = jnp.swapaxes(numer, 0, 1)
    packed = jnp.zeros((rows_here, cols_here), F32)
    for f in range(field_count + 1):
        if f < field_count:
            value = (numer[f] + area * land_flux[f]) / denom
            merged[f] = value
        else:
            value = kappa[...]
        edges[f] = jnp.concatenate([value[:EDGE], value[rows_here - EDGE :]], axis=0)
        strip = jnp.where(border, value, 0.0)
        packed = packed + (pltpu.roll(strip, f * LANE_BLOCK, 1) if f else strip)
    strips[...] = packed


def bin_all(arrays, picked, earlier, cap, rows_here):
    _, rows, field_count, cells = arrays[0].shape
    shape = (rows_here // TILE_ROWS * (TILE_ROWS + 1), field_count, ATM_COLS)
    number = sum(part[2] for pick in picked for part in pick)
    each = 2 * (field_count + 1) * TILE_ROWS * cells * ATM_COLS
    return pl.pallas_call(
        functools.partial(bin_slots, cap, picked, len(arrays)),
        out_shape=[jax.ShapeDtypeStruct(shape, F32)] * len(picked),
        in_specs=[VMEM] * (len(arrays) + len(earlier)),
        out_specs=[VMEM] * len(picked),
        compiler_params=params(),
        cost_estimate=pl.CostEstimate(
            flops=number * 8 * each,
            bytes_accessed=number * rows * field_count * cells * 2,
            transcendentals=0,
        ),
    )(*arrays, *earlier)


def merge(total, other, passed, land_flux, land_area, kappa):
    field_count, rows_here, cols_here = land_flux.shape
    return pl.pallas_call(
        merge_kernel,
        out_shape=[
            jax.ShapeDtypeStruct(land_flux.shape, F32),
            jax.ShapeDtypeStruct((rows_here, cols_here), F32),
            jax.ShapeDtypeStruct((field_count + 1, 2 * EDGE, cols_here), F32),
        ],
        in_specs=[VMEM] * 6,
        out_specs=[VMEM] * 3,
        compiler_params=params(),
    )(total, other, passed, land_flux, land_area, kappa)


def swaps(axis):
    count = lax.axis_size(axis)
    first = [(i, i ^ 1) for i in range(count) if i ^ 1 < count]
    second = [(i, i + 1) for i in range(1, count - 1, 2)]
    return first, second + [(b, a) for a, b in second]


def neighbours(values, axis):
    first, second = swaps(axis)
    one = lax.ppermute(values, axis, first)
    two = lax.ppermute(values, axis, second)
    odd = lax.axis_index(axis) % 2 == 1
    return jnp.where(odd, one, two), jnp.where(odd, two, one)


def select_columns(before, after):
    lane = (iota(before.shape, 1) + SWEEPS) % before.shape[1] % LANE_BLOCK
    return jnp.where(lane < SWEEPS, before, after)


def ends(values):
    rows = values.shape[0]
    return jnp.concatenate([values[:EDGE], values[rows - EDGE :]], axis=0)


def sweep_kernel(merged, before, after, above, below, kappa, out, held):
    field_count, rows_here, cols_here = merged.shape
    rows = rows_here + 2 * EDGE
    pad = (held.shape[1] - rows) // 2
    lane = iota((rows, cols_here), 1)
    border = (lane < SWEEPS) | (lane >= cols_here - SWEEPS)
    columns = jnp.concatenate(
        [
            above[field_count + 1][EDGE:],
            select_columns(before[...], after[...]),
            below[field_count + 1][:EDGE],
        ],
        axis=0,
    )

    def put(f, cells):
        held[f, pad : pad + rows] = cells

    def put_whole(f, cells):
        shift = (cols_here - f * LANE_BLOCK) % cols_here
        side = pltpu.roll(columns, shift, 1) if f else columns
        middle = jnp.concatenate([above[f][EDGE:], cells, below[f][:EDGE]], axis=0)
        put(f, jnp.concatenate([middle, jnp.where(border, side, 0.0)], axis=1))

    def neighbours_of(f, cells):
        return (
            held[f, pad - 1 : pad - 1 + rows],
            held[f, pad + 1 : pad + 1 + rows],
            pltpu.roll(cells, 2 * cols_here - 1, 1),
            pltpu.roll(cells, 1, 1),
        )

    empty = jnp.zeros((pad, 2 * cols_here), F32)
    for f in range(field_count + 1):
        held[f, :pad] = empty
        held[f, pad + rows :] = empty
        put_whole(f, merged[f] if f < field_count else kappa[...])

    k = held[field_count, pad : pad + rows]
    inside = k > 0.0
    coefficients = [
        jnp.where(inside, 0.5 * (k + near), 0.0) for near in neighbours_of(field_count, k)
    ]
    for sweep_index in range(SWEEPS):
        for f in range(field_count):
            u = held[f, pad : pad + rows]
            new = u
            for coefficient, near in zip(coefficients, neighbours_of(f, u), strict=True):
                new = new + coefficient * (near - u)
            if sweep_index < SWEEPS - 1:
                put(f, new)
            else:
                out[f] = new[EDGE : EDGE + rows_here, :cols_here]


def shards(
    ocean_fields,
    dest_device,
    dest_tile,
    cell_target,
    cell_weight,
    sea_mask,
    land_flux,
    land_area,
    kappa,
):
    tiles_here, field_count, tile_cells = ocean_fields.shape
    crossing_count = dest_device.shape[1]
    width_x = lax.axis_size("gx")
    width_y = lax.axis_size("gy")
    device_count = width_x * width_y
    cap = max(2, tiles_here * crossing_count * 2 // device_count)
    layer = width_x // LAYERS * width_y
    rows_here, cols_here = land_area.shape

    mirror = (LAYERS - 1) * layer
    pairs = (dest_device.T, dest_tile.T, cell_target, cell_weight, sea_mask, ocean_fields)
    halves = [
        [h * (device_count // 2) + i for i in range(device_count // 2)] for h in range(2)
    ]
    exchange = functools.partial(
        lax.all_to_all,
        axis_name=("gx", "gy"),
        split_axis=0,
        concat_axis=0,
        axis_index_groups=halves,
        tiled=True,
    )
    half = device_count // 2
    everywhere = range(device_count)
    far_slots = pack(*pairs, cap, device_count, False, mirror)[0]
    pairs, far_slots = lax.optimization_barrier((pairs, far_slots))
    far_got = exchange(far_slots)
    kept, given = pack(*pairs, cap, device_count, True, 0)
    taken = lax.ppermute(given, ("gx", "gy"), [(i, i ^ 1) for i in everywhere])
    messages = join(kept, taken)

    def deliver(j):
        pairing = [(i, i ^ 2 * carried(j, i & 1)) for i in everywhere]
        return lax.ppermute(messages[j], ("gx", "gy"), pairing)

    half_way = len(messages) // 2
    soon = [deliver(j) for j in reversed(range(half_way))]
    late = [deliver(j) for j in range(half_way, len(messages))]

    far_total = bin_all([far_got], [[(0, 0, half)]], [], cap, rows_here)[0]
    opposite = [(i, i ^ (mirror // width_y)) for i in range(width_x)]
    passed = lax.ppermute(far_total, "gx", opposite)

    def sums(messages, *which, earlier=()):
        picked = [[(j, 2 * i, 2) for j in range(len(messages))] for i in which]
        return bin_all(messages, picked, earlier, cap, rows_here)

    totals = []
    for message in soon:
        message, far_total = lax.optimization_barrier((message, far_total))
        totals = sums([message], 0, 1, earlier=totals)
        far_total = totals[0]
    own, other = totals
    late, own = lax.optimization_barrier((late, own))
    other = sums(late, 1, earlier=[other])[0]
    other = lax.ppermute(other, ("gx", "gy"), [(i, i ^ 1) for i in everywhere])
    own = sums(late, 0, earlier=[own])[0]

    merged, strips, edges = merge(own, other, passed, land_flux, land_area, kappa)
    before, after = neighbours(strips, "gx")
    corners = ends(select_columns(before, after))
    above, below = neighbours(jnp.concatenate([edges, corners[None]], axis=0), "gy")
    return pl.pallas_call(
        sweep_kernel,
        out_shape=jax.ShapeDtypeStruct(merged.shape, F32),
        in_specs=[VMEM] * 6,
        out_specs=VMEM,
        scratch_shapes=[
            pltpu.VMEM((field_count + 1, rows_here + 2 * EDGE + 16, 2 * cols_here), F32)
        ],
        compiler_params=params(),
    )(merged, before, after, above, below, kappa)


def solution(mesh):
    return jax.shard_map(
        shards,
        mesh=mesh,
        in_specs=(
            P(("gx", "gy"), None, None),
            P(("gx", "gy"), None),
            P(("gx", "gy"), None),
            P(("gx", "gy"), None, None),
            P(("gx", "gy"), None, None),
            P(("gx", "gy"), None),
            P(None, "gy", "gx"),
            P("gy", "gx"),
            P("gy", "gx"),
        ),
        out_specs=P(None, "gy", "gx"),
        check_vma=False,
    )
```

```python
import functools

import jax
import jax.numpy as jnp
from jax import lax
from jax.experimental import pallas as pl
from jax.experimental.pallas import tpu as pltpu
from jax.sharding import PartitionSpec as P

TILE_ROWS = 8
ATM_COLS = 128
COL_BITS = 7
SWEEPS = 3
LAYERS = 4
EDGE = 4
MEAN_SCALE = 2.0**8
WEIGHT_SCALE = 2.0**-2
TOGETHER = 8
LANE_BLOCK = 14

BF16 = jnp.bfloat16
F32 = jnp.float32
I32 = jnp.int32
VMEM = pl.BlockSpec(memory_space=pltpu.VMEM)
HBM = pl.BlockSpec(memory_space=pltpu.HBM)
ANY = pl.BlockSpec(memory_space=pl.ANY)


def iota(shape, dim):
    return lax.broadcasted_iota(I32, shape, dim)


def params(megabytes=40):
    return pltpu.CompilerParams(vmem_limit_bytes=megabytes << 20)


def parity(number):
    for shift in (16, 8, 4, 2, 1):
        number = number ^ (number >> shift)
    return number & 1


def swapped(position, core):
    return position ^ ((((position >> 1) - 1) >> 31) & 1 & (1 ^ core))


def carried(position, core):
    index = swapped(position, core)
    return 2 * index + (parity(index) ^ 1 ^ core)


def pack_kernel(cap, near, mirror, *refs):
    given, outs, held, out_held = refs[:7], refs[7:-12], refs[-12:-5], refs[-5]
    count, source, in_sems, out_sems = refs[-4:]
    copies = [
        pltpu.make_async_copy(given[i], held[i], in_sems.at[i]) for i in range(len(given))
    ]
    for i in (0, 6, 1, 2, 3, 4, 5):
        copies[i].start()
    dest_s, dest_v, tile_v, target, weight, mask, fields = held
    crossings, tiles = dest_v.shape
    half, cells = out_held.shape[0], fields.shape[2]
    owners, slots = 2 * half, half * cap
    me = lax.axis_index("gx") * lax.axis_size("gy") + lax.axis_index("gy")
    first = me // half * half
    here = me - first
    core = here & 1

    def block_of(owner):
        if not near:
            return (owner ^ mirror) - first
        index = owner - first
        distance = (index ^ here) >> 1
        carrier = 1 - parity(distance)
        position = swapped(distance >> 1, carrier)
        block = (carrier ^ core) * (half // 2) + position * 2 + ((index & 1) ^ carrier)
        return jnp.where((index >= 0) & (index < half), block, -1)

    def owner_of(block):
        if not near:
            return (first + block) ^ mirror
        carrier = core ^ (block // (half // 2))
        distance = carried((block % (half // 2)) >> 1, carrier)
        return first + (((here >> 1) ^ distance) << 1) + ((block & 1) ^ carrier)

    for d in range(owners):
        count[d] = 0

    def clear(i, carry):
        source[i] = 0
        return carry

    lax.fori_loop(0, owners * cap, clear, 0, unroll=16)
    copies[0].wait()
    for k in range(crossings):

        def enter(o, carry):
            d = dest_s[k, o]
            n = count[d]
            count[d] = n + 1
            source[d * cap + n] = o
            return carry

        lax.fori_loop(0, tiles, enter, 0, unroll=16)

    copies[6].wait()
    parts = out_sems.shape[0] // 2
    step = half // parts
    sent = []

    def send(part, rows):
        into = outs[part * step // outs[0].shape[0]]
        there = part * step % outs[0].shape[0]
        copy = pltpu.make_async_copy(
            out_held.at[pl.ds(part * step, step), rows],
            into.at[pl.ds(there, step), rows],
            out_sems.at[len(sent)],
        )
        copy.start()
        sent.append(copy)

    for part in range(parts):

        def fill(g, carry):
            owner = owner_of(g)
            for n in range(cap):
                out_held[g, n] = fields[source[owner * cap + n]]
            return carry

        lax.fori_loop(part * step, (part + 1) * step, fill, 0, unroll=2)
        send(part, pl.ds(0, cap))

    for copy in copies[1:6]:
        copy.wait()
    sea = mask[...] != 0
    every_weight = weight[...].astype(F32)
    before = (iota((tiles, tiles), 0) < iota((tiles, tiles), 1)).astype(BF16)
    offset = jnp.zeros((owners, 1), F32)
    packed_w = jnp.zeros((slots, cells), F32)
    packed_c = jnp.zeros((slots, cells), F32)
    for k in range(crossings):
        dest = dest_v[k : k + 1, :]
        hot = (iota((owners, tiles), 0) == dest).astype(F32)
        earlier = jnp.dot(hot.astype(BF16), before, preferred_element_type=F32) + offset
        offset = offset + jnp.sum(hot, axis=1, keepdims=True)
        within = jnp.sum(hot * earlier, axis=0, keepdims=True).astype(I32)
        chosen = (iota((slots, tiles), 0) == block_of(dest) * cap + within).astype(BF16)
        scale = jnp.ones(dest.shape, F32)
        for bit in (1, 2, 4):
            scale = scale * jnp.where((tile_v[k : k + 1, :] & bit) != 0, 2.0 ** (8 * bit), 1.0)
        cell = target[:, k, :]
        code = ((cell & (ATM_COLS - 1)) + ATM_COLS) << (cell >> COL_BITS)
        packed_w = packed_w + jnp.dot(
            chosen,
            jnp.where(sea, every_weight[:, k, :], 0.0).astype(BF16),
            preferred_element_type=F32,
        )
        packed_c = packed_c + jnp.dot(
            chosen * scale.astype(BF16), code.astype(F32).astype(BF16), preferred_element_type=F32
        )
    packed_w = packed_w.astype(BF16)
    packed_c = packed_c.astype(BF16)
    spare = jnp.zeros((8 - cap, cells), BF16)
    for g in range(half):
        for row, packed in ((cap, packed_w), (cap + 1, packed_c)):
            rows = packed[g * cap : (g + 1) * cap]
            out_held[g, row] = rows if cap == 8 else jnp.concatenate([rows, spare], axis=0)

    for part in range(parts):
        send(part, pl.ds(cap, 2))
    for copy in sent:
        copy.wait()


def pack(dest, tile, target, weight, mask, fields, cap, owners, near, mirror):
    half = owners // 2
    shape = (half, cap + 2) + fields.shape[1:]
    parts = 2 if near else 1
    given = (dest, dest, tile, target, weight, mask, fields)
    return pl.pallas_call(
        functools.partial(pack_kernel, cap, near, mirror),
        out_shape=[jax.ShapeDtypeStruct((half // parts,) + shape[1:], BF16)] * parts,
        in_specs=[HBM] * len(given),
        out_specs=[HBM] * parts,
        scratch_shapes=[pltpu.SMEM(dest.shape, I32)]
        + [pltpu.VMEM(a.shape, a.dtype) for a in given[1:]]
        + [
            pltpu.VMEM(shape, BF16),
            pltpu.SMEM((owners,), I32),
            pltpu.SMEM((owners * cap,), I32),
            pltpu.SemaphoreType.DMA((len(given),)),
            pltpu.SemaphoreType.DMA((8,)),
        ],
        compiler_params=params(62),
        cost_estimate=pl.CostEstimate(
            flops=10**8, bytes_accessed=4 * 10**6, transcendentals=0
        ),
    )(*given)


def join_kernel(kept, taken, *refs):
    outs, (held, in_sems, out_sems) = refs[:-3], refs[-3:]
    arriving = []
    for j in range(len(outs)):
        for rel in range(2):
            for src, blocks in enumerate((kept, taken)):
                at = 4 * j + 2 * rel + src
                copy = pltpu.make_async_copy(blocks.at[2 * j + rel], held.at[at], in_sems.at[at])
                copy.start()
                arriving.append(copy)
    leaving = []
    for j, out in enumerate(outs):
        for copy in arriving[4 * j : 4 * j + 4]:
            copy.wait()
        leaving.append(pltpu.make_async_copy(held.at[pl.ds(4 * j, 4)], out, out_sems.at[j]))
        leaving[-1].start()
    for copy in leaving:
        copy.wait()


def join(kept, taken):
    number = taken.shape[0] // 2
    return pl.pallas_call(
        join_kernel,
        out_shape=[jax.ShapeDtypeStruct((4,) + taken.shape[1:], BF16)] * number,
        in_specs=[HBM] * 2,
        out_specs=[HBM] * number,
        scratch_shapes=[
            pltpu.VMEM((4 * number,) + taken.shape[1:], BF16),
            pltpu.SemaphoreType.DMA((4 * number,)),
            pltpu.SemaphoreType.DMA((number,)),
        ],
        compiler_params=params(62),
        cost_estimate=pl.CostEstimate(
            flops=0, bytes_accessed=4 * taken.size * 2, transcendentals=0
        ),
    )(kept, taken)


def decode(code):
    tile = jnp.zeros(code.shape, I32)
    for k in range(1, 8):
        tile = tile + jnp.where(code >= 2.0 ** (7 + 8 * k), 1, 0)
    scaled = code
    for bit in (1, 2, 4):
        scaled = jnp.where((tile & bit) != 0, scaled * 2.0 ** (-8 * bit), scaled)
    cell = scaled.astype(I32)
    row = jnp.zeros(code.shape, I32)
    for k in range(1, 8):
        row = row + jnp.where(cell >= (1 << (7 + k)), 1, 0)
    return tile, row, lax.shift_right_logical(cell, row) - ATM_COLS


def bin_slots(cap, picked, arrays, averaged, *refs):
    given, before, totals = refs[:arrays], refs[arrays : -len(picked)], refs[-len(picked) :]
    for n, (pick, total) in enumerate(zip(picked, totals, strict=True)):
        total[...] = before[n][...] if before else jnp.zeros_like(total)
        for array, first, number in pick:
            together = min(number, TOGETHER)

            def some(i, carry):
                for block in range(together):
                    bin_block(cap, given[array], first + i * together + block, total)
                return carry

            lax.fori_loop(0, number // together, some, 0, unroll=number == together)
        if averaged:
            average(total)


def average(total):
    rows_here = total.shape[0] * TILE_ROWS // (TILE_ROWS + 1)
    for tile in range(rows_here // TILE_ROWS):
        weight = total[rows_here + tile]
        factor = jnp.where(weight > 0.0, MEAN_SCALE / weight, 0.0)
        for row in range(TILE_ROWS):
            total[tile * TILE_ROWS + row] = total[tile * TILE_ROWS + row] * factor[row : row + 1]
        total[rows_here + tile] = weight * WEIGHT_SCALE


def bin_block(cap, slots, i, total):
    field_count, cells = slots.shape[2:]
    rows_here = total.shape[0] * TILE_ROWS // (TILE_ROWS + 1)
    zero = jnp.zeros((), BF16)
    weight = slots[i, cap].astype(F32)
    tile, row, col = decode(slots[i, cap + 1].astype(F32))
    row16 = row.astype(F32).astype(BF16)
    col16 = col.astype(F32).astype(BF16)
    weight16 = weight.astype(BF16)
    for n in range(cap):
        field = slots[i, n]
        t = tile[n, 0]
        row_n = jnp.broadcast_to(row16[n : n + 1], (16, cells))
        twice = jnp.concatenate([field, field], axis=0)
        sub = iota((16, cells), 0)
        left = []
        for q in range(0, TILE_ROWS, 2):
            want = jnp.where(sub >= 8, q + 1.0, q + 0.0).astype(BF16)
            left.append(jnp.where(row_n == want, twice, zero))
        ones = jnp.ones((), BF16)
        left.append(jnp.where(row_n == sub.astype(F32).astype(BF16), ones, zero))
        right = jnp.where(
            jnp.broadcast_to(col16[n : n + 1], (ATM_COLS, cells))
            == iota((ATM_COLS, cells), 0).astype(F32).astype(BF16),
            jnp.broadcast_to(weight16[n : n + 1], (ATM_COLS, cells)),
            zero,
        )
        added = lax.dot_general(
            jnp.concatenate(left, axis=0),
            right,
            (((1,), (1,)), ((), ())),
            preferred_element_type=F32,
        )
        main = TILE_ROWS * field_count
        total[pl.ds(t * TILE_ROWS, TILE_ROWS)] += added[:main].reshape(
            TILE_ROWS, field_count, ATM_COLS
        )
        total[pl.ds(rows_here + t, 1)] += added[main : main + TILE_ROWS].reshape(
            1, TILE_ROWS, ATM_COLS
        )


def merge_kernel(total, other, passed, land_flux, land_area, kappa, merged, strips, edges):
    field_count, rows_here, cols_here = land_flux.shape
    area = land_area[...]
    weight = passed[rows_here:] * (1.0 / WEIGHT_SCALE)
    denom = total[rows_here:] + other[rows_here:] + weight
    denom = denom.reshape(rows_here, cols_here) + area
    lane = iota((rows_here, cols_here), 1)
    border = (lane < SWEEPS) | (lane >= cols_here - SWEEPS)
    weight = weight.reshape(rows_here, 1, cols_here) * (1.0 / MEAN_SCALE)
    numer = total[:rows_here] + other[:rows_here] + passed[:rows_here] * weight
    numer = jnp.swapaxes(numer, 0, 1)
    packed = jnp.zeros((rows_here, cols_here), F32)
    for f in range(field_count + 1):
        if f < field_count:
            value = (numer[f] + area * land_flux[f]) / denom
            merged[f] = value
        else:
            value = kappa[...]
        edges[f] = jnp.concatenate([value[:EDGE], value[rows_here - EDGE :]], axis=0)
        strip = jnp.where(border, value, 0.0)
        packed = packed + (pltpu.roll(strip, f * LANE_BLOCK, 1) if f else strip)
    strips[...] = packed


def bin_all(arrays, picked, earlier, cap, rows_here, averaged=False):
    _, rows, field_count, cells = arrays[0].shape
    shape = (rows_here // TILE_ROWS * (TILE_ROWS + 1), field_count, ATM_COLS)
    number = sum(part[2] for pick in picked for part in pick)
    each = 2 * (field_count + 1) * TILE_ROWS * cells * ATM_COLS
    return pl.pallas_call(
        functools.partial(bin_slots, cap, picked, len(arrays), averaged),
        out_shape=[jax.ShapeDtypeStruct(shape, F32)] * len(picked),
        in_specs=[VMEM] * (len(arrays) + len(earlier)),
        out_specs=[VMEM] * len(picked),
        compiler_params=params(),
        cost_estimate=pl.CostEstimate(
            flops=number * 8 * each if averaged else 0,
            bytes_accessed=number * rows * field_count * cells * 2 if averaged else 0,
            transcendentals=0,
        ),
    )(*arrays, *earlier)


def merge(total, other, passed, land_flux, land_area, kappa):
    field_count, rows_here, cols_here = land_flux.shape
    return pl.pallas_call(
        merge_kernel,
        out_shape=[
            jax.ShapeDtypeStruct(land_flux.shape, F32),
            jax.ShapeDtypeStruct((rows_here, cols_here), F32),
            jax.ShapeDtypeStruct((field_count + 1, 2 * EDGE, cols_here), F32),
        ],
        in_specs=[VMEM] * 6,
        out_specs=[VMEM] * 3,
        compiler_params=params(),
    )(total, other, passed, land_flux, land_area, kappa)


def swaps(axis):
    count = lax.axis_size(axis)
    first = [(i, i ^ 1) for i in range(count) if i ^ 1 < count]
    second = [(i, i + 1) for i in range(1, count - 1, 2)]
    return first, second + [(b, a) for a, b in second]


def neighbours(values, axis):
    first, second = swaps(axis)
    one = lax.ppermute(values, axis, first)
    two = lax.ppermute(values, axis, second)
    odd = lax.axis_index(axis) % 2 == 1
    return jnp.where(odd, one, two), jnp.where(odd, two, one)


def select_columns(before, after):
    lane = (iota(before.shape, 1) + SWEEPS) % before.shape[1] % LANE_BLOCK
    return jnp.where(lane < SWEEPS, before, after)


def ends(values):
    rows = values.shape[0]
    return jnp.concatenate([values[:EDGE], values[rows - EDGE :]], axis=0)


def sweep_kernel(merged, before, after, above, below, kappa, out, held):
    field_count, rows_here, cols_here = merged.shape
    rows = rows_here + 2 * EDGE
    pad = (held.shape[1] - rows) // 2
    lane = iota((rows, cols_here), 1)
    border = (lane < SWEEPS) | (lane >= cols_here - SWEEPS)
    columns = jnp.concatenate(
        [
            above[field_count + 1][EDGE:],
            select_columns(before[...], after[...]),
            below[field_count + 1][:EDGE],
        ],
        axis=0,
    )

    def put(f, cells):
        held[f, pad : pad + rows] = cells

    def put_whole(f, cells):
        shift = (cols_here - f * LANE_BLOCK) % cols_here
        side = pltpu.roll(columns, shift, 1) if f else columns
        middle = jnp.concatenate([above[f][EDGE:], cells, below[f][:EDGE]], axis=0)
        put(f, jnp.concatenate([middle, jnp.where(border, side, 0.0)], axis=1))

    def neighbours_of(f, cells):
        return (
            held[f, pad - 1 : pad - 1 + rows],
            held[f, pad + 1 : pad + 1 + rows],
            pltpu.roll(cells, 2 * cols_here - 1, 1),
            pltpu.roll(cells, 1, 1),
        )

    empty = jnp.zeros((pad, 2 * cols_here), F32)
    for f in range(field_count + 1):
        held[f, :pad] = empty
        held[f, pad + rows :] = empty
        put_whole(f, merged[f] if f < field_count else kappa[...])

    k = held[field_count, pad : pad + rows]
    inside = k > 0.0
    coefficients = [
        jnp.where(inside, 0.5 * (k + near), 0.0) for near in neighbours_of(field_count, k)
    ]
    for sweep_index in range(SWEEPS):
        for f in range(field_count):
            u = held[f, pad : pad + rows]
            new = u
            for coefficient, near in zip(coefficients, neighbours_of(f, u), strict=True):
                new = new + coefficient * (near - u)
            if sweep_index < SWEEPS - 1:
                put(f, new)
            else:
                out[f] = new[EDGE : EDGE + rows_here, :cols_here]


def shards(
    ocean_fields,
    dest_device,
    dest_tile,
    cell_target,
    cell_weight,
    sea_mask,
    land_flux,
    land_area,
    kappa,
):
    tiles_here, field_count, tile_cells = ocean_fields.shape
    crossing_count = dest_device.shape[1]
    width_x = lax.axis_size("gx")
    width_y = lax.axis_size("gy")
    device_count = width_x * width_y
    cap = max(2, tiles_here * crossing_count * 2 // device_count)
    layer = width_x // LAYERS * width_y
    rows_here, cols_here = land_area.shape

    mirror = (LAYERS - 1) * layer
    pairs = (dest_device.T, dest_tile.T, cell_target, cell_weight, sea_mask, ocean_fields)
    halves = [
        [h * (device_count // 2) + i for i in range(device_count // 2)] for h in range(2)
    ]
    exchange = functools.partial(
        lax.all_to_all,
        axis_name=("gx", "gy"),
        split_axis=0,
        concat_axis=0,
        axis_index_groups=halves,
        tiled=True,
    )
    half = device_count // 2
    everywhere = range(device_count)
    far_slots = pack(*pairs, cap, device_count, False, mirror)[0]
    pairs, far_slots = lax.optimization_barrier((pairs, far_slots))
    far_got = exchange(far_slots)
    kept, given = pack(*pairs, cap, device_count, True, 0)
    taken = lax.ppermute(given, ("gx", "gy"), [(i, i ^ 1) for i in everywhere])
    messages = join(kept, taken)

    def deliver(j):
        pairing = [(i, i ^ 2 * carried(j, i & 1)) for i in everywhere]
        return lax.ppermute(messages[j], ("gx", "gy"), pairing)

    half_way = len(messages) // 2
    soon = [deliver(j) for j in range(half_way)]
    late = [deliver(j) for j in range(half_way, len(messages))]

    far_total = bin_all([far_got], [[(0, 0, half)]], [], cap, rows_here, averaged=True)[0]
    opposite = [(i, i ^ (mirror // width_y)) for i in range(width_x)]
    passed = lax.ppermute(far_total.astype(jnp.float16), "gx", opposite).astype(F32)

    def sums(messages, *which, earlier=()):
        picked = [[(j, 2 * i, 2) for j in range(len(messages))] for i in which]
        return bin_all(messages, picked, earlier, cap, rows_here)

    totals = []
    for message in soon:
        message, far_total = lax.optimization_barrier((message, far_total))
        totals = sums([message], 0, 1, earlier=totals)
        far_total = totals[0]
    own, other = totals
    late, own, passed = lax.optimization_barrier((late, own, passed))
    other = sums(late, 1, earlier=[other])[0]
    other = lax.ppermute(other, ("gx", "gy"), [(i, i ^ 1) for i in everywhere])
    own = sums(late, 0, earlier=[own])[0]

    merged, strips, edges = merge(own, other, passed, land_flux, land_area, kappa)
    before, after = neighbours(strips, "gx")
    corners = ends(select_columns(before, after))
    above, below = neighbours(jnp.concatenate([edges, corners[None]], axis=0), "gy")
    return pl.pallas_call(
        sweep_kernel,
        out_shape=jax.ShapeDtypeStruct(merged.shape, F32),
        in_specs=[VMEM] * 6,
        out_specs=VMEM,
        scratch_shapes=[
            pltpu.VMEM((field_count + 1, rows_here + 2 * EDGE + 16, 2 * cols_here), F32)
        ],
        compiler_params=params(),
    )(merged, before, after, above, below, kappa)


def solution(mesh):
    return jax.shard_map(
        shards,
        mesh=mesh,
        in_specs=(
            P(("gx", "gy"), None, None),
            P(("gx", "gy"), None),
            P(("gx", "gy"), None),
            P(("gx", "gy"), None, None),
            P(("gx", "gy"), None, None),
            P(("gx", "gy"), None),
            P(None, "gy", "gx"),
            P("gy", "gx"),
            P("gy", "gx"),
        ),
        out_specs=P(None, "gy", "gx"),
        check_vma=False,
    )
```

```python
import functools

import jax
import jax.numpy as jnp
from jax import lax
from jax.experimental import pallas as pl
from jax.experimental.pallas import tpu as pltpu
from jax.sharding import PartitionSpec as P

TILE_ROWS = 8
ATM_COLS = 128
COL_BITS = 7
SWEEPS = 3
LAYERS = 4
EDGE = 4
MEAN_SCALE = 2.0**13
WEIGHT_SCALE = 2.0**-2
PART = 4
TOGETHER = 8
LANE_BLOCK = 14

BF16 = jnp.bfloat16
F32 = jnp.float32
I32 = jnp.int32
VMEM = pl.BlockSpec(memory_space=pltpu.VMEM)
HBM = pl.BlockSpec(memory_space=pltpu.HBM)
ANY = pl.BlockSpec(memory_space=pl.ANY)


def iota(shape, dim):
    return lax.broadcasted_iota(I32, shape, dim)


def params(megabytes=40):
    return pltpu.CompilerParams(vmem_limit_bytes=megabytes << 20)


def parity(number):
    for shift in (16, 8, 4, 2, 1):
        number = number ^ (number >> shift)
    return number & 1


def swapped(position, core):
    return position ^ ((((position >> 1) - 1) >> 31) & 1 & (1 ^ core))


def carried(position, core):
    index = swapped(position, core)
    return 2 * index + (parity(index) ^ 1 ^ core)


def pack_kernel(cap, near, mirror, *refs):
    if near:
        given, outs, held = refs[:7], refs[7:-10], refs[-10:-3]
        count, source, in_sems = refs[-3:]
        blocks = outs
    else:
        given, out, held = refs[:7], refs[7], refs[8:15]
        out_held, count, source, in_sems, out_sems = refs[15:]
        blocks = [out_held.at[pl.ds(i * PART, PART)] for i in range(out.shape[0] // PART)]
    copies = [
        pltpu.make_async_copy(given[i], held[i], in_sems.at[i]) for i in range(len(given))
    ]
    for i in (0, 6, 1, 2, 3, 4, 5):
        copies[i].start()
    dest_s, dest_v, tile_v, target, weight, mask, fields = held
    crossings, tiles = dest_v.shape
    step = blocks[0].shape[0]
    half, cells = len(blocks) * step, fields.shape[2]
    owners, slots = 2 * half, half * cap
    me = lax.axis_index("gx") * lax.axis_size("gy") + lax.axis_index("gy")
    first = me // half * half
    here = me - first
    core = here & 1

    def block_of(owner):
        if not near:
            return (owner ^ mirror) - first
        index = owner - first
        distance = (index ^ here) >> 1
        carrier = 1 - parity(distance)
        position = swapped(distance >> 1, carrier)
        block = (carrier ^ core) * (half // 2) + position * 2 + ((index & 1) ^ carrier)
        return jnp.where((index >= 0) & (index < half), block, -1)

    def owner_of(block):
        if not near:
            return (first + block) ^ mirror
        carrier = core ^ (block // (half // 2))
        distance = carried((block % (half // 2)) >> 1, carrier)
        return first + (((here >> 1) ^ distance) << 1) + ((block & 1) ^ carrier)

    for d in range(owners):
        count[d] = 0

    def clear(i, carry):
        source[i] = 0
        return carry

    lax.fori_loop(0, owners * cap, clear, 0, unroll=16)
    copies[0].wait()
    for k in range(crossings):

        def enter(o, carry):
            d = dest_s[k, o]
            n = count[d]
            count[d] = n + 1
            source[d * cap + n] = o
            return carry

        lax.fori_loop(0, tiles, enter, 0, unroll=16)

    copies[6].wait()
    sent = []

    def send(part, rows):
        if near:
            return
        into = out.at[pl.ds(part * step, step), rows]
        copy = pltpu.make_async_copy(blocks[part].at[:, rows], into, out_sems.at[len(sent)])
        copy.start()
        sent.append(copy)

    for part, block in enumerate(blocks):

        def fill(g, carry):
            owner = owner_of(part * step + g)
            for n in range(cap):
                block[g, n] = fields[source[owner * cap + n]]
            return carry

        lax.fori_loop(0, step, fill, 0, unroll=2)
        send(part, pl.ds(0, cap))

    for copy in copies[1:6]:
        copy.wait()
    sea = mask[...] != 0
    every_weight = weight[...].astype(F32)
    before = (iota((tiles, tiles), 0) < iota((tiles, tiles), 1)).astype(BF16)
    offset = jnp.zeros((owners, 1), F32)
    packed_w = jnp.zeros((slots, cells), F32)
    packed_c = jnp.zeros((slots, cells), F32)
    for k in range(crossings):
        dest = dest_v[k : k + 1, :]
        hot = (iota((owners, tiles), 0) == dest).astype(F32)
        earlier = jnp.dot(hot.astype(BF16), before, preferred_element_type=F32) + offset
        offset = offset + jnp.sum(hot, axis=1, keepdims=True)
        within = jnp.sum(hot * earlier, axis=0, keepdims=True).astype(I32)
        chosen = (iota((slots, tiles), 0) == block_of(dest) * cap + within).astype(BF16)
        scale = jnp.ones(dest.shape, F32)
        for bit in (1, 2, 4):
            scale = scale * jnp.where((tile_v[k : k + 1, :] & bit) != 0, 2.0 ** (8 * bit), 1.0)
        cell = target[:, k, :]
        code = ((cell & (ATM_COLS - 1)) + ATM_COLS) << (cell >> COL_BITS)
        packed_w = packed_w + jnp.dot(
            chosen,
            jnp.where(sea, every_weight[:, k, :], 0.0).astype(BF16),
            preferred_element_type=F32,
        )
        packed_c = packed_c + jnp.dot(
            chosen * scale.astype(BF16), code.astype(F32).astype(BF16), preferred_element_type=F32
        )
    packed_w = packed_w.astype(BF16)
    packed_c = packed_c.astype(BF16)
    spare = jnp.zeros((8 - cap, cells), BF16)
    for g in range(half):
        for row, packed in ((cap, packed_w), (cap + 1, packed_c)):
            rows = packed[g * cap : (g + 1) * cap]
            rows = rows if cap == 8 else jnp.concatenate([rows, spare], axis=0)
            blocks[g // step][g % step, row] = rows

    for part in range(len(blocks)):
        send(part, pl.ds(cap, 2))
    for copy in sent:
        copy.wait()


def pack(dest, tile, target, weight, mask, fields, cap, owners, near, mirror):
    half = owners // 2
    shape = (half, cap + 2) + fields.shape[1:]
    parts = 2 if near else 1
    given = (dest, dest, tile, target, weight, mask, fields)
    scratch = [pltpu.SMEM(dest.shape, I32)] + [pltpu.VMEM(a.shape, a.dtype) for a in given[1:]]
    if not near:
        scratch.append(pltpu.VMEM(shape, BF16))
    scratch += [
        pltpu.SMEM((owners,), I32),
        pltpu.SMEM((owners * cap,), I32),
        pltpu.SemaphoreType.DMA((len(given),)),
    ]
    if not near:
        scratch.append(pltpu.SemaphoreType.DMA((2 * (half // PART),)))
    return pl.pallas_call(
        functools.partial(pack_kernel, cap, near, mirror),
        out_shape=[jax.ShapeDtypeStruct((half // parts,) + shape[1:], BF16)] * parts,
        in_specs=[HBM] * len(given),
        out_specs=[VMEM if near else HBM] * parts,
        scratch_shapes=scratch,
        compiler_params=params(50 if near else 62),
        cost_estimate=pl.CostEstimate(
            flops=10**8, bytes_accessed=4 * 10**6, transcendentals=0
        ),
    )(*given)


def join_kernel(kept, taken, *outs):
    for j, out in enumerate(outs):
        for rel in range(2):
            out[2 * rel] = kept[2 * j + rel]
            out[2 * rel + 1] = taken[2 * j + rel]


def join(kept, taken):
    number = taken.shape[0] // 2
    return pl.pallas_call(
        join_kernel,
        out_shape=[jax.ShapeDtypeStruct((4,) + taken.shape[1:], BF16)] * number,
        in_specs=[VMEM] * 2,
        out_specs=[VMEM] * number,
        compiler_params=params(),
        cost_estimate=pl.CostEstimate(
            flops=0, bytes_accessed=4 * taken.size * 2, transcendentals=0
        ),
    )(kept, taken)


def decode(code):
    tile = jnp.zeros(code.shape, I32)
    for k in range(1, 8):
        tile = tile + jnp.where(code >= 2.0 ** (7 + 8 * k), 1, 0)
    scaled = code
    for bit in (1, 2, 4):
        scaled = jnp.where((tile & bit) != 0, scaled * 2.0 ** (-8 * bit), scaled)
    cell = scaled.astype(I32)
    row = jnp.zeros(code.shape, I32)
    for k in range(1, 8):
        row = row + jnp.where(cell >= (1 << (7 + k)), 1, 0)
    return tile, row, lax.shift_right_logical(cell, row) - ATM_COLS


def bin_slots(cap, picked, arrays, averaged, *refs):
    given, before, totals = refs[:arrays], refs[arrays : -len(picked)], refs[-len(picked) :]
    for n, (pick, total) in enumerate(zip(picked, totals, strict=True)):
        total[...] = before[n][...] if before else jnp.zeros_like(total)
        for array, first, number in pick:
            together = min(number, TOGETHER)

            def some(i, carry):
                for block in range(together):
                    bin_block(cap, given[array], first + i * together + block, total)
                return carry

            lax.fori_loop(0, number // together, some, 0, unroll=number == together)
        if averaged:
            average(total)


def average(total):
    rows_here = total.shape[0] * TILE_ROWS // (TILE_ROWS + 1)
    for tile in range(rows_here // TILE_ROWS):
        weight = total[rows_here + tile]
        factor = jnp.where(weight > 0.0, MEAN_SCALE / weight, 0.0)
        for row in range(TILE_ROWS):
            total[tile * TILE_ROWS + row] = total[tile * TILE_ROWS + row] * factor[row : row + 1]
        total[rows_here + tile] = weight * WEIGHT_SCALE


def bin_block(cap, slots, i, total):
    field_count, cells = slots.shape[2:]
    rows_here = total.shape[0] * TILE_ROWS // (TILE_ROWS + 1)
    zero = jnp.zeros((), BF16)
    weight = slots[i, cap].astype(F32)
    tile, row, col = decode(slots[i, cap + 1].astype(F32))
    row16 = row.astype(F32).astype(BF16)
    col16 = col.astype(F32).astype(BF16)
    weight16 = weight.astype(BF16)
    for n in range(cap):
        field = slots[i, n]
        t = tile[n, 0]
        row_n = jnp.broadcast_to(row16[n : n + 1], (16, cells))
        twice = jnp.concatenate([field, field], axis=0)
        sub = iota((16, cells), 0)
        left = []
        for q in range(0, TILE_ROWS, 2):
            want = jnp.where(sub >= 8, q + 1.0, q + 0.0).astype(BF16)
            left.append(jnp.where(row_n == want, twice, zero))
        ones = jnp.ones((), BF16)
        left.append(jnp.where(row_n == sub.astype(F32).astype(BF16), ones, zero))
        right = jnp.where(
            jnp.broadcast_to(col16[n : n + 1], (ATM_COLS, cells))
            == iota((ATM_COLS, cells), 0).astype(F32).astype(BF16),
            jnp.broadcast_to(weight16[n : n + 1], (ATM_COLS, cells)),
            zero,
        )
        added = lax.dot_general(
            jnp.concatenate(left, axis=0),
            right,
            (((1,), (1,)), ((), ())),
            preferred_element_type=F32,
        )
        main = TILE_ROWS * field_count
        total[pl.ds(t * TILE_ROWS, TILE_ROWS)] += added[:main].reshape(
            TILE_ROWS, field_count, ATM_COLS
        )
        total[pl.ds(rows_here + t, 1)] += added[main : main + TILE_ROWS].reshape(
            1, TILE_ROWS, ATM_COLS
        )


def merge_kernel(total, other, passed, land_flux, land_area, kappa, merged, strips, edges):
    field_count, rows_here, cols_here = land_flux.shape
    area = land_area[...]
    weight = passed[rows_here:] * (1.0 / WEIGHT_SCALE)
    denom = total[rows_here:] + other[rows_here:] + weight
    denom = denom.reshape(rows_here, cols_here) + area
    lane = iota((rows_here, cols_here), 1)
    border = (lane < SWEEPS) | (lane >= cols_here - SWEEPS)
    weight = weight.reshape(rows_here, 1, cols_here) * (1.0 / MEAN_SCALE)
    numer = total[:rows_here] + other[:rows_here] + passed[:rows_here] * weight
    numer = jnp.swapaxes(numer, 0, 1)
    packed = jnp.zeros((rows_here, cols_here), F32)
    for f in range(field_count + 1):
        if f < field_count:
            value = (numer[f] + area * land_flux[f]) / denom
            merged[f] = value
        else:
            value = kappa[...]
        edges[f] = jnp.concatenate([value[:EDGE], value[rows_here - EDGE :]], axis=0)
        strip = jnp.where(border, value, 0.0)
        packed = packed + (pltpu.roll(strip, f * LANE_BLOCK, 1) if f else strip)
    strips[...] = packed


def bin_all(arrays, picked, earlier, cap, rows_here, averaged=False):
    _, rows, field_count, cells = arrays[0].shape
    shape = (rows_here // TILE_ROWS * (TILE_ROWS + 1), field_count, ATM_COLS)
    number = sum(part[2] for pick in picked for part in pick)
    each = 2 * (field_count + 1) * TILE_ROWS * cells * ATM_COLS
    return pl.pallas_call(
        functools.partial(bin_slots, cap, picked, len(arrays), averaged),
        out_shape=[jax.ShapeDtypeStruct(shape, F32)] * len(picked),
        in_specs=[VMEM] * (len(arrays) + len(earlier)),
        out_specs=[VMEM] * len(picked),
        compiler_params=params(),
        cost_estimate=pl.CostEstimate(
            flops=number * 8 * each if averaged else 0,
            bytes_accessed=number * rows * field_count * cells * 2 if averaged else 0,
            transcendentals=0,
        ),
    )(*arrays, *earlier)


def merge(total, other, passed, land_flux, land_area, kappa):
    field_count, rows_here, cols_here = land_flux.shape
    return pl.pallas_call(
        merge_kernel,
        out_shape=[
            jax.ShapeDtypeStruct(land_flux.shape, F32),
            jax.ShapeDtypeStruct((rows_here, cols_here), F32),
            jax.ShapeDtypeStruct((field_count + 1, 2 * EDGE, cols_here), F32),
        ],
        in_specs=[VMEM] * 6,
        out_specs=[VMEM] * 3,
        compiler_params=params(),
    )(total, other, passed, land_flux, land_area, kappa)


def swaps(axis):
    count = lax.axis_size(axis)
    first = [(i, i ^ 1) for i in range(count) if i ^ 1 < count]
    second = [(i, i + 1) for i in range(1, count - 1, 2)]
    return first, second + [(b, a) for a, b in second]


def neighbours(values, axis):
    first, second = swaps(axis)
    one = lax.ppermute(values, axis, first)
    two = lax.ppermute(values, axis, second)
    odd = lax.axis_index(axis) % 2 == 1
    return jnp.where(odd, one, two), jnp.where(odd, two, one)


def select_columns(before, after):
    lane = (iota(before.shape, 1) + SWEEPS) % before.shape[1] % LANE_BLOCK
    return jnp.where(lane < SWEEPS, before, after)


def ends(values):
    rows = values.shape[0]
    return jnp.concatenate([values[:EDGE], values[rows - EDGE :]], axis=0)


def sweep_kernel(merged, before, after, above, below, kappa, out, held):
    field_count, rows_here, cols_here = merged.shape
    rows = rows_here + 2 * EDGE
    pad = (held.shape[1] - rows) // 2
    lane = iota((rows, cols_here), 1)
    border = (lane < SWEEPS) | (lane >= cols_here - SWEEPS)
    columns = jnp.concatenate(
        [
            above[field_count + 1][EDGE:],
            select_columns(before[...], after[...]),
            below[field_count + 1][:EDGE],
        ],
        axis=0,
    )

    def put(f, cells):
        held[f, pad : pad + rows] = cells

    def put_whole(f, cells):
        shift = (cols_here - f * LANE_BLOCK) % cols_here
        side = pltpu.roll(columns, shift, 1) if f else columns
        middle = jnp.concatenate([above[f][EDGE:], cells, below[f][:EDGE]], axis=0)
        put(f, jnp.concatenate([middle, jnp.where(border, side, 0.0)], axis=1))

    def neighbours_of(f, cells):
        return (
            held[f, pad - 1 : pad - 1 + rows],
            held[f, pad + 1 : pad + 1 + rows],
            pltpu.roll(cells, 2 * cols_here - 1, 1),
            pltpu.roll(cells, 1, 1),
        )

    empty = jnp.zeros((pad, 2 * cols_here), F32)
    for f in range(field_count + 1):
        held[f, :pad] = empty
        held[f, pad + rows :] = empty
        put_whole(f, merged[f] if f < field_count else kappa[...])

    k = held[field_count, pad : pad + rows]
    inside = k > 0.0
    coefficients = [
        jnp.where(inside, 0.5 * (k + near), 0.0) for near in neighbours_of(field_count, k)
    ]
    for sweep_index in range(SWEEPS):
        for f in range(field_count):
            u = held[f, pad : pad + rows]
            new = u
            for coefficient, near in zip(coefficients, neighbours_of(f, u), strict=True):
                new = new + coefficient * (near - u)
            if sweep_index < SWEEPS - 1:
                put(f, new)
            else:
                out[f] = new[EDGE : EDGE + rows_here, :cols_here]


def shards(
    ocean_fields,
    dest_device,
    dest_tile,
    cell_target,
    cell_weight,
    sea_mask,
    land_flux,
    land_area,
    kappa,
):
    tiles_here, field_count, tile_cells = ocean_fields.shape
    crossing_count = dest_device.shape[1]
    width_x = lax.axis_size("gx")
    width_y = lax.axis_size("gy")
    device_count = width_x * width_y
    cap = max(2, tiles_here * crossing_count * 2 // device_count)
    layer = width_x // LAYERS * width_y
    rows_here, cols_here = land_area.shape

    mirror = (LAYERS - 1) * layer
    pairs = (dest_device.T, dest_tile.T, cell_target, cell_weight, sea_mask, ocean_fields)
    halves = [
        [h * (device_count // 2) + i for i in range(device_count // 2)] for h in range(2)
    ]
    exchange = functools.partial(
        lax.all_to_all,
        axis_name=("gx", "gy"),
        split_axis=0,
        concat_axis=0,
        axis_index_groups=halves,
        tiled=True,
    )
    half = device_count // 2
    everywhere = range(device_count)
    far_slots = pack(*pairs, cap, device_count, False, mirror)[0]
    pairs, far_slots = lax.optimization_barrier((pairs, far_slots))
    far_got = exchange(far_slots)
    kept, given = pack(*pairs, cap, device_count, True, 0)
    taken = lax.ppermute(given, ("gx", "gy"), [(i, i ^ 1) for i in everywhere])
    messages = join(kept, taken)

    def deliver(j):
        pairing = [(i, i ^ 2 * carried(j, i & 1)) for i in everywhere]
        return lax.ppermute(messages[j], ("gx", "gy"), pairing)

    soon = [deliver(j) for j in range(0, len(messages), 2)]
    late = [deliver(j) for j in range(1, len(messages), 2)]

    far_total = bin_all([far_got], [[(0, 0, half)]], [], cap, rows_here, averaged=True)[0]
    opposite = [(i, i ^ (mirror // width_y)) for i in range(width_x)]
    passed = lax.ppermute(far_total.astype(jnp.float16), "gx", opposite).astype(F32)

    def sums(messages, *which, earlier=()):
        picked = [[(j, 2 * i, 2) for j in range(len(messages))] for i in which]
        return bin_all(messages, picked, earlier, cap, rows_here)

    totals = []
    for message in soon:
        message, far_total = lax.optimization_barrier((message, far_total))
        totals = sums([message], 0, 1, earlier=totals)
        far_total = totals[0]
    own, other = totals
    late, own = lax.optimization_barrier((late, own))
    other = sums(late, 1, earlier=[other])[0]
    other, passed = lax.optimization_barrier((other, passed))
    other = lax.ppermute(other, ("gx", "gy"), [(i, i ^ 1) for i in everywhere])
    own = sums(late, 0, earlier=[own])[0]

    merged, strips, edges = merge(own, other, passed, land_flux, land_area, kappa)
    before, after = neighbours(strips, "gx")
    corners = ends(select_columns(before, after))
    above, below = neighbours(jnp.concatenate([edges, corners[None]], axis=0), "gy")
    return pl.pallas_call(
        sweep_kernel,
        out_shape=jax.ShapeDtypeStruct(merged.shape, F32),
        in_specs=[VMEM] * 6,
        out_specs=VMEM,
        scratch_shapes=[
            pltpu.VMEM((field_count + 1, rows_here + 2 * EDGE + 16, 2 * cols_here), F32)
        ],
        compiler_params=params(),
    )(merged, before, after, above, below, kappa)


def solution(mesh):
    return jax.shard_map(
        shards,
        mesh=mesh,
        in_specs=(
            P(("gx", "gy"), None, None),
            P(("gx", "gy"), None),
            P(("gx", "gy"), None),
            P(("gx", "gy"), None, None),
            P(("gx", "gy"), None, None),
            P(("gx", "gy"), None),
            P(None, "gy", "gx"),
            P("gy", "gx"),
            P("gy", "gx"),
        ),
        out_specs=P(None, "gy", "gx"),
        check_vma=False,
    )
```

```python
import functools

import jax
import jax.numpy as jnp
from jax import lax
from jax.experimental import pallas as pl
from jax.experimental.pallas import tpu as pltpu
from jax.sharding import PartitionSpec as P

TILE_ROWS = 8
ATM_COLS = 128
COL_BITS = 7
SWEEPS = 3
LAYERS = 4
EDGE = 4
MEAN_SCALE = 2.0**13
WEIGHT_SCALE = 2.0**-2
PART = 4
TOGETHER = 8
LANE_BLOCK = 14

BF16 = jnp.bfloat16
F32 = jnp.float32
I32 = jnp.int32
VMEM = pl.BlockSpec(memory_space=pltpu.VMEM)
HBM = pl.BlockSpec(memory_space=pltpu.HBM)
ANY = pl.BlockSpec(memory_space=pl.ANY)


def iota(shape, dim):
    return lax.broadcasted_iota(I32, shape, dim)


def params(megabytes=40):
    return pltpu.CompilerParams(vmem_limit_bytes=megabytes << 20)


def parity(number):
    for shift in (16, 8, 4, 2, 1):
        number = number ^ (number >> shift)
    return number & 1


def swapped(position, core):
    return position ^ ((((position >> 1) - 1) >> 31) & 1 & (1 ^ core))


def carried(position, core):
    index = swapped(position, core)
    return 2 * index + (parity(index) ^ 1 ^ core)


def pack_kernel(cap, near, mirror, *refs):
    if near:
        given, outs, held = refs[:7], refs[7:-10], refs[-10:-3]
        count, source, in_sems = refs[-3:]
        blocks = outs
    else:
        given, out, held = refs[:7], refs[7], refs[8:15]
        out_held, count, source, in_sems, out_sems = refs[15:]
        blocks = [out_held.at[pl.ds(i * PART, PART)] for i in range(out.shape[0] // PART)]
    copies = [
        pltpu.make_async_copy(given[i], held[i], in_sems.at[i]) for i in range(len(given))
    ]
    for i in (0, 6, 1, 2, 3, 4, 5):
        copies[i].start()
    dest_s, dest_v, tile_v, target, weight, mask, fields = held
    crossings, tiles = dest_v.shape
    step = blocks[0].shape[0]
    half, cells = len(blocks) * step, fields.shape[2]
    owners, slots = 2 * half, half * cap
    me = lax.axis_index("gx") * lax.axis_size("gy") + lax.axis_index("gy")
    first = me // half * half
    here = me - first
    core = here & 1

    def block_of(owner):
        if not near:
            return (owner ^ mirror) - first
        index = owner - first
        distance = (index ^ here) >> 1
        carrier = 1 - parity(distance)
        position = swapped(distance >> 1, carrier)
        block = (carrier ^ core) * (half // 2) + position * 2 + ((index & 1) ^ carrier)
        return jnp.where((index >= 0) & (index < half), block, -1)

    def owner_of(block):
        if not near:
            return (first + block) ^ mirror
        carrier = core ^ (block // (half // 2))
        distance = carried((block % (half // 2)) >> 1, carrier)
        return first + (((here >> 1) ^ distance) << 1) + ((block & 1) ^ carrier)

    for d in range(owners):
        count[d] = 0

    def clear(i, carry):
        source[i] = 0
        return carry

    lax.fori_loop(0, owners * cap, clear, 0, unroll=16)
    copies[0].wait()
    for k in range(crossings):

        def enter(o, carry):
            d = dest_s[k, o]
            n = count[d]
            count[d] = n + 1
            source[d * cap + n] = o
            return carry

        lax.fori_loop(0, tiles, enter, 0, unroll=16)

    copies[6].wait()
    sent = []

    def send(part, rows):
        if near:
            return
        into = out.at[pl.ds(part * step, step), rows]
        copy = pltpu.make_async_copy(blocks[part].at[:, rows], into, out_sems.at[len(sent)])
        copy.start()
        sent.append(copy)

    for part, block in enumerate(blocks):

        def fill(g, carry):
            owner = owner_of(part * step + g)
            for n in range(cap):
                block[g, n] = fields[source[owner * cap + n]]
            return carry

        lax.fori_loop(0, step, fill, 0, unroll=2)
        send(part, pl.ds(0, cap))

    for copy in copies[1:6]:
        copy.wait()
    sea = mask[...] != 0
    every_weight = weight[...].astype(F32)
    before = (iota((tiles, tiles), 0) < iota((tiles, tiles), 1)).astype(BF16)
    offset = jnp.zeros((owners, 1), F32)
    packed_w = jnp.zeros((slots, cells), F32)
    packed_c = jnp.zeros((slots, cells), F32)
    for k in range(crossings):
        dest = dest_v[k : k + 1, :]
        hot = (iota((owners, tiles), 0) == dest).astype(F32)
        earlier = jnp.dot(hot.astype(BF16), before, preferred_element_type=F32) + offset
        offset = offset + jnp.sum(hot, axis=1, keepdims=True)
        within = jnp.sum(hot * earlier, axis=0, keepdims=True).astype(I32)
        chosen = (iota((slots, tiles), 0) == block_of(dest) * cap + within).astype(BF16)
        scale = jnp.ones(dest.shape, F32)
        for bit in (1, 2, 4):
            scale = scale * jnp.where((tile_v[k : k + 1, :] & bit) != 0, 2.0 ** (8 * bit), 1.0)
        cell = target[:, k, :]
        code = ((cell & (ATM_COLS - 1)) + ATM_COLS) << (cell >> COL_BITS)
        packed_w = packed_w + jnp.dot(
            chosen,
            jnp.where(sea, every_weight[:, k, :], 0.0).astype(BF16),
            preferred_element_type=F32,
        )
        packed_c = packed_c + jnp.dot(
            chosen * scale.astype(BF16), code.astype(F32).astype(BF16), preferred_element_type=F32
        )
    packed_w = packed_w.astype(BF16)
    packed_c = packed_c.astype(BF16)
    spare = jnp.zeros((8 - cap, cells), BF16)
    for g in range(half):
        for row, packed in ((cap, packed_w), (cap + 1, packed_c)):
            rows = packed[g * cap : (g + 1) * cap]
            rows = rows if cap == 8 else jnp.concatenate([rows, spare], axis=0)
            blocks[g // step][g % step, row] = rows

    for part in range(len(blocks)):
        send(part, pl.ds(cap, 2))
    for copy in sent:
        copy.wait()


def pack(dest, tile, target, weight, mask, fields, cap, owners, near, mirror):
    half = owners // 2
    shape = (half, cap + 2) + fields.shape[1:]
    parts = 2 if near else 1
    given = (dest, dest, tile, target, weight, mask, fields)
    scratch = [pltpu.SMEM(dest.shape, I32)] + [pltpu.VMEM(a.shape, a.dtype) for a in given[1:]]
    if not near:
        scratch.append(pltpu.VMEM(shape, BF16))
    scratch += [
        pltpu.SMEM((owners,), I32),
        pltpu.SMEM((owners * cap,), I32),
        pltpu.SemaphoreType.DMA((len(given),)),
    ]
    if not near:
        scratch.append(pltpu.SemaphoreType.DMA((2 * (half // PART),)))
    return pl.pallas_call(
        functools.partial(pack_kernel, cap, near, mirror),
        out_shape=[jax.ShapeDtypeStruct((half // parts,) + shape[1:], BF16)] * parts,
        in_specs=[HBM] * len(given),
        out_specs=[VMEM if near else HBM] * parts,
        scratch_shapes=scratch,
        compiler_params=params(50 if near else 62),
        cost_estimate=pl.CostEstimate(
            flops=10**8, bytes_accessed=4 * 10**6, transcendentals=0
        ),
    )(*given)


def join_kernel(kept, taken, *outs):
    for j, out in enumerate(outs):
        for rel in range(2):
            out[2 * rel] = kept[2 * j + rel]
            out[2 * rel + 1] = taken[2 * j + rel]


def join(kept, taken):
    number = taken.shape[0] // 2
    return pl.pallas_call(
        join_kernel,
        out_shape=[jax.ShapeDtypeStruct((4,) + taken.shape[1:], BF16)] * number,
        in_specs=[VMEM] * 2,
        out_specs=[VMEM] * number,
        compiler_params=params(),
        cost_estimate=pl.CostEstimate(
            flops=0, bytes_accessed=4 * taken.size * 2, transcendentals=0
        ),
    )(kept, taken)


def decode(code):
    tile = jnp.zeros(code.shape, I32)
    for k in range(1, 8):
        tile = tile + jnp.where(code >= 2.0 ** (7 + 8 * k), 1, 0)
    scaled = code
    for bit in (1, 2, 4):
        scaled = jnp.where((tile & bit) != 0, scaled * 2.0 ** (-8 * bit), scaled)
    cell = scaled.astype(I32)
    row = jnp.zeros(code.shape, I32)
    for k in range(1, 8):
        row = row + jnp.where(cell >= (1 << (7 + k)), 1, 0)
    return tile, row, lax.shift_right_logical(cell, row) - ATM_COLS


def bin_slots(cap, picked, arrays, averaged, *refs):
    given, before, totals = refs[:arrays], refs[arrays : -len(picked)], refs[-len(picked) :]
    for n, (pick, total) in enumerate(zip(picked, totals, strict=True)):
        total[...] = before[n][...] if before else jnp.zeros_like(total)
        for array, first, number in pick:
            together = min(number, TOGETHER)

            def some(i, carry):
                for block in range(together):
                    bin_block(cap, given[array], first + i * together + block, total)
                return carry

            lax.fori_loop(0, number // together, some, 0, unroll=number == together)
        if averaged:
            average(total)


def average(total):
    rows_here = total.shape[0] * TILE_ROWS // (TILE_ROWS + 1)
    for tile in range(rows_here // TILE_ROWS):
        weight = total[rows_here + tile]
        factor = jnp.where(weight > 0.0, MEAN_SCALE / weight, 0.0)
        for row in range(TILE_ROWS):
            total[tile * TILE_ROWS + row] = total[tile * TILE_ROWS + row] * factor[row : row + 1]
        total[rows_here + tile] = weight * WEIGHT_SCALE


def bin_block(cap, slots, i, total):
    field_count, cells = slots.shape[2:]
    rows_here = total.shape[0] * TILE_ROWS // (TILE_ROWS + 1)
    zero = jnp.zeros((), BF16)
    weight = slots[i, cap].astype(F32)
    tile, row, col = decode(slots[i, cap + 1].astype(F32))
    row16 = row.astype(F32).astype(BF16)
    col16 = col.astype(F32).astype(BF16)
    weight16 = weight.astype(BF16)
    for n in range(cap):
        field = slots[i, n]
        t = tile[n, 0]
        row_n = jnp.broadcast_to(row16[n : n + 1], (16, cells))
        twice = jnp.concatenate([field, field], axis=0)
        sub = iota((16, cells), 0)
        left = []
        for q in range(0, TILE_ROWS, 2):
            want = jnp.where(sub >= 8, q + 1.0, q + 0.0).astype(BF16)
            left.append(jnp.where(row_n == want, twice, zero))
        ones = jnp.ones((), BF16)
        left.append(jnp.where(row_n == sub.astype(F32).astype(BF16), ones, zero))
        right = jnp.where(
            jnp.broadcast_to(col16[n : n + 1], (ATM_COLS, cells))
            == iota((ATM_COLS, cells), 0).astype(F32).astype(BF16),
            jnp.broadcast_to(weight16[n : n + 1], (ATM_COLS, cells)),
            zero,
        )
        added = lax.dot_general(
            jnp.concatenate(left, axis=0),
            right,
            (((1,), (1,)), ((), ())),
            preferred_element_type=F32,
        )
        main = TILE_ROWS * field_count
        total[pl.ds(t * TILE_ROWS, TILE_ROWS)] += added[:main].reshape(
            TILE_ROWS, field_count, ATM_COLS
        )
        total[pl.ds(rows_here + t, 1)] += added[main : main + TILE_ROWS].reshape(
            1, TILE_ROWS, ATM_COLS
        )


def merge_kernel(total, other, passed, land_flux, land_area, kappa, merged, strips, edges):
    field_count, rows_here, cols_here = land_flux.shape
    area = land_area[...]
    weight = passed[rows_here:] * (1.0 / WEIGHT_SCALE)
    denom = total[rows_here:] + other[rows_here:] + weight
    denom = denom.reshape(rows_here, cols_here) + area
    lane = iota((rows_here, cols_here), 1)
    border = (lane < SWEEPS) | (lane >= cols_here - SWEEPS)
    weight = weight.reshape(rows_here, 1, cols_here) * (1.0 / MEAN_SCALE)
    numer = total[:rows_here] + other[:rows_here] + passed[:rows_here] * weight
    numer = jnp.swapaxes(numer, 0, 1)
    packed = jnp.zeros((rows_here, cols_here), F32)
    for f in range(field_count + 1):
        if f < field_count:
            value = (numer[f] + area * land_flux[f]) / denom
            merged[f] = value
        else:
            value = kappa[...]
        edges[f] = jnp.concatenate([value[:EDGE], value[rows_here - EDGE :]], axis=0)
        strip = jnp.where(border, value, 0.0)
        packed = packed + (pltpu.roll(strip, f * LANE_BLOCK, 1) if f else strip)
    strips[...] = packed


def bin_all(arrays, picked, earlier, cap, rows_here, averaged=False):
    _, rows, field_count, cells = arrays[0].shape
    shape = (rows_here // TILE_ROWS * (TILE_ROWS + 1), field_count, ATM_COLS)
    number = sum(part[2] for pick in picked for part in pick)
    each = 2 * (field_count + 1) * TILE_ROWS * cells * ATM_COLS
    return pl.pallas_call(
        functools.partial(bin_slots, cap, picked, len(arrays), averaged),
        out_shape=[jax.ShapeDtypeStruct(shape, F32)] * len(picked),
        in_specs=[VMEM] * (len(arrays) + len(earlier)),
        out_specs=[VMEM] * len(picked),
        compiler_params=params(),
        cost_estimate=pl.CostEstimate(
            flops=number * 8 * each if averaged else 0,
            bytes_accessed=number * rows * field_count * cells * 2 if averaged else 0,
            transcendentals=0,
        ),
    )(*arrays, *earlier)


def merge(total, other, passed, land_flux, land_area, kappa):
    field_count, rows_here, cols_here = land_flux.shape
    return pl.pallas_call(
        merge_kernel,
        out_shape=[
            jax.ShapeDtypeStruct(land_flux.shape, F32),
            jax.ShapeDtypeStruct((rows_here, cols_here), F32),
            jax.ShapeDtypeStruct((field_count + 1, 2 * EDGE, cols_here), F32),
        ],
        in_specs=[VMEM] * 6,
        out_specs=[VMEM] * 3,
        compiler_params=params(),
    )(total, other, passed, land_flux, land_area, kappa)


def swaps(axis):
    count = lax.axis_size(axis)
    first = [(i, i ^ 1) for i in range(count) if i ^ 1 < count]
    second = [(i, i + 1) for i in range(1, count - 1, 2)]
    return first, second + [(b, a) for a, b in second]


def neighbours(values, axis):
    first, second = swaps(axis)
    one = lax.ppermute(values, axis, first)
    two = lax.ppermute(values, axis, second)
    odd = lax.axis_index(axis) % 2 == 1
    return jnp.where(odd, one, two), jnp.where(odd, two, one)


def select_columns(before, after):
    lane = (iota(before.shape, 1) + SWEEPS) % before.shape[1] % LANE_BLOCK
    return jnp.where(lane < SWEEPS, before, after)


def ends(values):
    rows = values.shape[0]
    return jnp.concatenate([values[:EDGE], values[rows - EDGE :]], axis=0)


def sweep_kernel(merged, before, after, above, below, kappa, out, held):
    field_count, rows_here, cols_here = merged.shape
    rows = rows_here + 2 * EDGE
    pad = (held.shape[1] - rows) // 2
    lane = iota((rows, cols_here), 1)
    border = (lane < SWEEPS) | (lane >= cols_here - SWEEPS)
    columns = jnp.concatenate(
        [
            above[field_count + 1][EDGE:],
            select_columns(before[...], after[...]),
            below[field_count + 1][:EDGE],
        ],
        axis=0,
    )

    def put(f, cells):
        held[f, pad : pad + rows] = cells

    def put_whole(f, cells):
        shift = (cols_here - f * LANE_BLOCK) % cols_here
        side = pltpu.roll(columns, shift, 1) if f else columns
        middle = jnp.concatenate([above[f][EDGE:], cells, below[f][:EDGE]], axis=0)
        put(f, jnp.concatenate([middle, jnp.where(border, side, 0.0)], axis=1))

    def neighbours_of(f, cells):
        return (
            held[f, pad - 1 : pad - 1 + rows],
            held[f, pad + 1 : pad + 1 + rows],
            pltpu.roll(cells, 2 * cols_here - 1, 1),
            pltpu.roll(cells, 1, 1),
        )

    empty = jnp.zeros((pad, 2 * cols_here), F32)
    for f in range(field_count + 1):
        held[f, :pad] = empty
        held[f, pad + rows :] = empty
        put_whole(f, merged[f] if f < field_count else kappa[...])

    k = held[field_count, pad : pad + rows]
    inside = k > 0.0
    coefficients = [
        jnp.where(inside, 0.5 * (k + near), 0.0) for near in neighbours_of(field_count, k)
    ]
    for sweep_index in range(SWEEPS):
        for f in range(field_count):
            u = held[f, pad : pad + rows]
            new = u
            for coefficient, near in zip(coefficients, neighbours_of(f, u), strict=True):
                new = new + coefficient * (near - u)
            if sweep_index < SWEEPS - 1:
                put(f, new)
            else:
                out[f] = new[EDGE : EDGE + rows_here, :cols_here]


def shards(
    ocean_fields,
    dest_device,
    dest_tile,
    cell_target,
    cell_weight,
    sea_mask,
    land_flux,
    land_area,
    kappa,
):
    tiles_here, field_count, tile_cells = ocean_fields.shape
    crossing_count = dest_device.shape[1]
    width_x = lax.axis_size("gx")
    width_y = lax.axis_size("gy")
    device_count = width_x * width_y
    cap = max(2, tiles_here * crossing_count * 2 // device_count)
    layer = width_x // LAYERS * width_y
    rows_here, cols_here = land_area.shape

    mirror = LAYERS // 2 * layer
    pairs = (dest_device.T, dest_tile.T, cell_target, cell_weight, sea_mask, ocean_fields)
    halves = [
        [h * (device_count // 2) + i for i in range(device_count // 2)] for h in range(2)
    ]
    exchange = functools.partial(
        lax.all_to_all,
        axis_name=("gx", "gy"),
        split_axis=0,
        concat_axis=0,
        axis_index_groups=halves,
        tiled=True,
    )
    half = device_count // 2
    everywhere = range(device_count)
    far_slots = pack(*pairs, cap, device_count, False, mirror)[0]
    pairs, far_slots = lax.optimization_barrier((pairs, far_slots))
    far_got = exchange(far_slots)
    kept, given = pack(*pairs, cap, device_count, True, 0)
    taken = lax.ppermute(given, ("gx", "gy"), [(i, i ^ 1) for i in everywhere])
    messages = join(kept, taken)

    def deliver(j):
        pairing = [(i, i ^ 2 * carried(j, i & 1)) for i in everywhere]
        return lax.ppermute(messages[j], ("gx", "gy"), pairing)

    soon = [deliver(j) for j in reversed(range(0, len(messages), 2))]
    late = [deliver(j) for j in range(1, len(messages), 2)]

    far_total = bin_all([far_got], [[(0, 0, half)]], [], cap, rows_here, averaged=True)[0]
    opposite = [(i, i ^ (mirror // width_y)) for i in range(width_x)]
    passed = lax.ppermute(far_total.astype(jnp.float16), "gx", opposite).astype(F32)

    def sums(messages, *which, earlier=()):
        picked = [[(j, 2 * i, 2) for j in range(len(messages))] for i in which]
        return bin_all(messages, picked, earlier, cap, rows_here)

    totals = []
    for message in soon:
        message, far_total = lax.optimization_barrier((message, far_total))
        totals = sums([message], 0, 1, earlier=totals)
        far_total = totals[0]
    own, other = totals
    late, own = lax.optimization_barrier((late, own))
    other = sums(late, 1, earlier=[other])[0]
    other, passed = lax.optimization_barrier((other, passed))
    other = lax.ppermute(other, ("gx", "gy"), [(i, i ^ 1) for i in everywhere])
    own = sums(late, 0, earlier=[own])[0]

    merged, strips, edges = merge(own, other, passed, land_flux, land_area, kappa)
    before, after = neighbours(strips, "gx")
    corners = ends(select_columns(before, after))
    above, below = neighbours(jnp.concatenate([edges, corners[None]], axis=0), "gy")
    return pl.pallas_call(
        sweep_kernel,
        out_shape=jax.ShapeDtypeStruct(merged.shape, F32),
        in_specs=[VMEM] * 6,
        out_specs=VMEM,
        scratch_shapes=[
            pltpu.VMEM((field_count + 1, rows_here + 2 * EDGE + 16, 2 * cols_here), F32)
        ],
        compiler_params=params(),
    )(merged, before, after, above, below, kappa)


def solution(mesh):
    return jax.shard_map(
        shards,
        mesh=mesh,
        in_specs=(
            P(("gx", "gy"), None, None),
            P(("gx", "gy"), None),
            P(("gx", "gy"), None),
            P(("gx", "gy"), None, None),
            P(("gx", "gy"), None, None),
            P(("gx", "gy"), None),
            P(None, "gy", "gx"),
            P("gy", "gx"),
            P("gy", "gx"),
        ),
        out_specs=P(None, "gy", "gx"),
        check_vma=False,
    )
```

```python
import functools

import jax
import jax.numpy as jnp
from jax import lax
from jax.experimental import pallas as pl
from jax.experimental.pallas import tpu as pltpu
from jax.sharding import PartitionSpec as P

TILE_ROWS = 8
ATM_COLS = 128
COL_BITS = 7
SWEEPS = 3
LAYERS = 4
EDGE = 4
MEAN_SCALE = 2.0**13
WEIGHT_SCALE = 2.0**-2
PART = 4
TOGETHER = 8
LANE_BLOCK = 14

BF16 = jnp.bfloat16
F32 = jnp.float32
I32 = jnp.int32
VMEM = pl.BlockSpec(memory_space=pltpu.VMEM)
HBM = pl.BlockSpec(memory_space=pltpu.HBM)
ANY = pl.BlockSpec(memory_space=pl.ANY)


def iota(shape, dim):
    return lax.broadcasted_iota(I32, shape, dim)


def params(megabytes=40):
    return pltpu.CompilerParams(vmem_limit_bytes=megabytes << 20)


def parity(number):
    for shift in (16, 8, 4, 2, 1):
        number = number ^ (number >> shift)
    return number & 1


def swapped(position, core):
    return position ^ ((((position >> 1) - 1) >> 31) & 1 & (1 ^ core))


def carried(position, core):
    index = swapped(position, core)
    return 2 * index + (parity(index) ^ 1 ^ core)


def pack_kernel(cap, near, mirror, *refs):
    if near:
        given, outs, held = refs[:7], refs[7:-10], refs[-10:-3]
        count, source, in_sems = refs[-3:]
        blocks = outs
    else:
        given, out, held = refs[:7], refs[7], refs[8:15]
        out_held, count, source, in_sems, out_sems = refs[15:]
        blocks = [out_held.at[pl.ds(i * PART, PART)] for i in range(out.shape[0] // PART)]
    copies = [
        pltpu.make_async_copy(given[i], held[i], in_sems.at[i]) for i in range(len(given))
    ]
    for i in (0, 6, 1, 2, 3, 4, 5):
        copies[i].start()
    dest_s, dest_v, tile_v, target, weight, mask, fields = held
    crossings, tiles = dest_v.shape
    step = blocks[0].shape[0]
    half, cells = len(blocks) * step, fields.shape[2]
    owners, slots = 2 * half, half * cap
    me = lax.axis_index("gx") * lax.axis_size("gy") + lax.axis_index("gy")
    first = me // half * half
    here = me - first
    core = here & 1

    def block_of(owner):
        if not near:
            return (owner ^ mirror) - first
        index = owner - first
        distance = (index ^ here) >> 1
        carrier = 1 - parity(distance)
        position = swapped(distance >> 1, carrier)
        block = (carrier ^ core) * (half // 2) + position * 2 + ((index & 1) ^ carrier)
        return jnp.where((index >= 0) & (index < half), block, -1)

    def owner_of(block):
        if not near:
            return (first + block) ^ mirror
        carrier = core ^ (block // (half // 2))
        distance = carried((block % (half // 2)) >> 1, carrier)
        return first + (((here >> 1) ^ distance) << 1) + ((block & 1) ^ carrier)

    for d in range(owners):
        count[d] = 0

    def clear(i, carry):
        source[i] = 0
        return carry

    lax.fori_loop(0, owners * cap, clear, 0, unroll=16)
    copies[0].wait()
    for k in range(crossings):

        def enter(o, carry):
            d = dest_s[k, o]
            n = count[d]
            count[d] = n + 1
            source[d * cap + n] = o
            return carry

        lax.fori_loop(0, tiles, enter, 0, unroll=16)

    copies[6].wait()
    sent = []

    def send(part, rows):
        if near:
            return
        into = out.at[pl.ds(part * step, step), rows]
        copy = pltpu.make_async_copy(blocks[part].at[:, rows], into, out_sems.at[len(sent)])
        copy.start()
        sent.append(copy)

    for part, block in enumerate(blocks):

        def fill(g, carry):
            owner = owner_of(part * step + g)
            for n in range(cap):
                block[g, n] = fields[source[owner * cap + n]]
            return carry

        lax.fori_loop(0, step, fill, 0, unroll=2)
        send(part, pl.ds(0, cap))

    for copy in copies[1:6]:
        copy.wait()
    sea = mask[...] != 0
    every_weight = weight[...].astype(F32)
    before = (iota((tiles, tiles), 0) < iota((tiles, tiles), 1)).astype(BF16)
    offset = jnp.zeros((owners, 1), F32)
    packed_w = jnp.zeros((slots, cells), F32)
    packed_c = jnp.zeros((slots, cells), F32)
    for k in range(crossings):
        dest = dest_v[k : k + 1, :]
        hot = (iota((owners, tiles), 0) == dest).astype(F32)
        earlier = jnp.dot(hot.astype(BF16), before, preferred_element_type=F32) + offset
        offset = offset + jnp.sum(hot, axis=1, keepdims=True)
        within = jnp.sum(hot * earlier, axis=0, keepdims=True).astype(I32)
        chosen = (iota((slots, tiles), 0) == block_of(dest) * cap + within).astype(BF16)
        scale = jnp.ones(dest.shape, F32)
        for bit in (1, 2, 4):
            scale = scale * jnp.where((tile_v[k : k + 1, :] & bit) != 0, 2.0 ** (8 * bit), 1.0)
        cell = target[:, k, :]
        code = ((cell & (ATM_COLS - 1)) + ATM_COLS) << (cell >> COL_BITS)
        packed_w = packed_w + jnp.dot(
            chosen,
            jnp.where(sea, every_weight[:, k, :], 0.0).astype(BF16),
            preferred_element_type=F32,
        )
        packed_c = packed_c + jnp.dot(
            chosen * scale.astype(BF16), code.astype(F32).astype(BF16), preferred_element_type=F32
        )
    packed_w = packed_w.astype(BF16)
    packed_c = packed_c.astype(BF16)
    spare = jnp.zeros((8 - cap, cells), BF16)
    for g in range(half):
        for row, packed in ((cap, packed_w), (cap + 1, packed_c)):
            rows = packed[g * cap : (g + 1) * cap]
            rows = rows if cap == 8 else jnp.concatenate([rows, spare], axis=0)
            blocks[g // step][g % step, row] = rows

    for part in range(len(blocks)):
        send(part, pl.ds(cap, 2))
    for copy in sent:
        copy.wait()


def pack(dest, tile, target, weight, mask, fields, cap, owners, near, mirror):
    half = owners // 2
    shape = (half, cap + 2) + fields.shape[1:]
    parts = 2 if near else 1
    given = (dest, dest, tile, target, weight, mask, fields)
    scratch = [pltpu.SMEM(dest.shape, I32)] + [pltpu.VMEM(a.shape, a.dtype) for a in given[1:]]
    if not near:
        scratch.append(pltpu.VMEM(shape, BF16))
    scratch += [
        pltpu.SMEM((owners,), I32),
        pltpu.SMEM((owners * cap,), I32),
        pltpu.SemaphoreType.DMA((len(given),)),
    ]
    if not near:
        scratch.append(pltpu.SemaphoreType.DMA((2 * (half // PART),)))
    return pl.pallas_call(
        functools.partial(pack_kernel, cap, near, mirror),
        out_shape=[jax.ShapeDtypeStruct((half // parts,) + shape[1:], BF16)] * parts,
        in_specs=[HBM] * len(given),
        out_specs=[VMEM if near else HBM] * parts,
        scratch_shapes=scratch,
        compiler_params=params(50 if near else 62),
        cost_estimate=pl.CostEstimate(
            flops=10**8, bytes_accessed=4 * 10**6, transcendentals=0
        ),
    )(*given)


def join_kernel(kept, taken, *outs):
    for j, out in enumerate(outs):
        for rel in range(2):
            out[2 * rel] = kept[2 * j + rel]
            out[2 * rel + 1] = taken[2 * j + rel]


def join(kept, taken):
    number = taken.shape[0] // 2
    return pl.pallas_call(
        join_kernel,
        out_shape=[jax.ShapeDtypeStruct((4,) + taken.shape[1:], BF16)] * number,
        in_specs=[VMEM] * 2,
        out_specs=[VMEM] * number,
        compiler_params=params(),
        cost_estimate=pl.CostEstimate(
            flops=0, bytes_accessed=4 * taken.size * 2, transcendentals=0
        ),
    )(kept, taken)


def decode(code):
    tile = jnp.zeros(code.shape, I32)
    for k in range(1, 8):
        tile = tile + jnp.where(code >= 2.0 ** (7 + 8 * k), 1, 0)
    scaled = code
    for bit in (1, 2, 4):
        scaled = jnp.where((tile & bit) != 0, scaled * 2.0 ** (-8 * bit), scaled)
    cell = scaled.astype(I32)
    row = jnp.zeros(code.shape, I32)
    for k in range(1, 8):
        row = row + jnp.where(cell >= (1 << (7 + k)), 1, 0)
    return tile, row, lax.shift_right_logical(cell, row) - ATM_COLS


def bin_slots(cap, picked, arrays, averaged, *refs):
    given, before, totals = refs[:arrays], refs[arrays : -len(picked)], refs[-len(picked) :]
    for n, (pick, total) in enumerate(zip(picked, totals, strict=True)):
        total[...] = before[n][...] if before else jnp.zeros_like(total)
        for array, first, number in pick:
            together = min(number, TOGETHER)

            def some(i, carry):
                for block in range(together):
                    bin_block(cap, given[array], first + i * together + block, total)
                return carry

            lax.fori_loop(0, number // together, some, 0, unroll=number == together)
        if averaged:
            average(total)


def average(total):
    rows_here = total.shape[0] * TILE_ROWS // (TILE_ROWS + 1)
    for tile in range(rows_here // TILE_ROWS):
        weight = total[rows_here + tile]
        factor = jnp.where(weight > 0.0, MEAN_SCALE / weight, 0.0)
        for row in range(TILE_ROWS):
            total[tile * TILE_ROWS + row] = total[tile * TILE_ROWS + row] * factor[row : row + 1]
        total[rows_here + tile] = weight * WEIGHT_SCALE


def bin_block(cap, slots, i, total):
    field_count, cells = slots.shape[2:]
    rows_here = total.shape[0] * TILE_ROWS // (TILE_ROWS + 1)
    zero = jnp.zeros((), BF16)
    weight = slots[i, cap].astype(F32)
    tile, row, col = decode(slots[i, cap + 1].astype(F32))
    row16 = row.astype(F32).astype(BF16)
    col16 = col.astype(F32).astype(BF16)
    weight16 = weight.astype(BF16)
    for n in range(cap):
        field = slots[i, n]
        t = tile[n, 0]
        row_n = jnp.broadcast_to(row16[n : n + 1], (16, cells))
        twice = jnp.concatenate([field, field], axis=0)
        sub = iota((16, cells), 0)
        left = []
        for q in range(0, TILE_ROWS, 2):
            want = jnp.where(sub >= 8, q + 1.0, q + 0.0).astype(BF16)
            left.append(jnp.where(row_n == want, twice, zero))
        ones = jnp.ones((), BF16)
        left.append(jnp.where(row_n == sub.astype(F32).astype(BF16), ones, zero))
        right = jnp.where(
            jnp.broadcast_to(col16[n : n + 1], (ATM_COLS, cells))
            == iota((ATM_COLS, cells), 0).astype(F32).astype(BF16),
            jnp.broadcast_to(weight16[n : n + 1], (ATM_COLS, cells)),
            zero,
        )
        added = lax.dot_general(
            jnp.concatenate(left, axis=0),
            right,
            (((1,), (1,)), ((), ())),
            preferred_element_type=F32,
        )
        main = TILE_ROWS * field_count
        total[pl.ds(t * TILE_ROWS, TILE_ROWS)] += added[:main].reshape(
            TILE_ROWS, field_count, ATM_COLS
        )
        total[pl.ds(rows_here + t, 1)] += added[main : main + TILE_ROWS].reshape(
            1, TILE_ROWS, ATM_COLS
        )


def merge_kernel(total, other, passed, land_flux, land_area, kappa, merged, strips, edges):
    field_count, rows_here, cols_here = land_flux.shape
    area = land_area[...]
    weight = passed[rows_here:] * (1.0 / WEIGHT_SCALE)
    denom = total[rows_here:] + other[rows_here:] + weight
    denom = denom.reshape(rows_here, cols_here) + area
    lane = iota((rows_here, cols_here), 1)
    border = (lane < SWEEPS) | (lane >= cols_here - SWEEPS)
    weight = weight.reshape(rows_here, 1, cols_here) * (1.0 / MEAN_SCALE)
    numer = total[:rows_here] + other[:rows_here] + passed[:rows_here] * weight
    numer = jnp.swapaxes(numer, 0, 1)
    packed = jnp.zeros((rows_here, cols_here), F32)
    for f in range(field_count + 1):
        if f < field_count:
            value = (numer[f] + area * land_flux[f]) / denom
            merged[f] = value
        else:
            value = kappa[...]
        edges[f] = jnp.concatenate([value[:EDGE], value[rows_here - EDGE :]], axis=0)
        strip = jnp.where(border, value, 0.0)
        packed = packed + (pltpu.roll(strip, f * LANE_BLOCK, 1) if f else strip)
    strips[...] = packed


def bin_all(arrays, picked, earlier, cap, rows_here, averaged=False):
    _, rows, field_count, cells = arrays[0].shape
    shape = (rows_here // TILE_ROWS * (TILE_ROWS + 1), field_count, ATM_COLS)
    number = sum(part[2] for pick in picked for part in pick)
    each = 2 * (field_count + 1) * TILE_ROWS * cells * ATM_COLS
    return pl.pallas_call(
        functools.partial(bin_slots, cap, picked, len(arrays), averaged),
        out_shape=[jax.ShapeDtypeStruct(shape, F32)] * len(picked),
        in_specs=[VMEM] * (len(arrays) + len(earlier)),
        out_specs=[VMEM] * len(picked),
        compiler_params=params(),
        cost_estimate=pl.CostEstimate(
            flops=number * 8 * each if averaged else 0,
            bytes_accessed=number * rows * field_count * cells * 2 if averaged else 0,
            transcendentals=0,
        ),
    )(*arrays, *earlier)


def merge(total, other, passed, land_flux, land_area, kappa):
    field_count, rows_here, cols_here = land_flux.shape
    return pl.pallas_call(
        merge_kernel,
        out_shape=[
            jax.ShapeDtypeStruct(land_flux.shape, F32),
            jax.ShapeDtypeStruct((rows_here, cols_here), F32),
            jax.ShapeDtypeStruct((field_count + 1, 2 * EDGE, cols_here), F32),
        ],
        in_specs=[VMEM] * 6,
        out_specs=[VMEM] * 3,
        compiler_params=params(),
    )(total, other, passed, land_flux, land_area, kappa)


def swaps(axis):
    count = lax.axis_size(axis)
    first = [(i, i ^ 1) for i in range(count) if i ^ 1 < count]
    second = [(i, i + 1) for i in range(1, count - 1, 2)]
    return first, second + [(b, a) for a, b in second]


def neighbours(values, axis):
    first, second = swaps(axis)
    one = lax.ppermute(values, axis, first)
    two = lax.ppermute(values, axis, second)
    odd = lax.axis_index(axis) % 2 == 1
    return jnp.where(odd, one, two), jnp.where(odd, two, one)


def select_columns(before, after):
    lane = (iota(before.shape, 1) + SWEEPS) % before.shape[1] % LANE_BLOCK
    return jnp.where(lane < SWEEPS, before, after)


def ends(values):
    rows = values.shape[0]
    return jnp.concatenate([values[:EDGE], values[rows - EDGE :]], axis=0)


def sweep_kernel(merged, before, after, above, below, kappa, out, held):
    field_count, rows_here, cols_here = merged.shape
    rows = rows_here + 2 * EDGE
    pad = (held.shape[1] - rows) // 2
    lane = iota((rows, cols_here), 1)
    border = (lane < SWEEPS) | (lane >= cols_here - SWEEPS)
    columns = jnp.concatenate(
        [
            above[field_count + 1][EDGE:],
            select_columns(before[...], after[...]),
            below[field_count + 1][:EDGE],
        ],
        axis=0,
    )

    def put(f, cells):
        held[f, pad : pad + rows] = cells

    def put_whole(f, cells):
        shift = (cols_here - f * LANE_BLOCK) % cols_here
        side = pltpu.roll(columns, shift, 1) if f else columns
        middle = jnp.concatenate([above[f][EDGE:], cells, below[f][:EDGE]], axis=0)
        put(f, jnp.concatenate([middle, jnp.where(border, side, 0.0)], axis=1))

    def neighbours_of(f, cells):
        return (
            held[f, pad - 1 : pad - 1 + rows],
            held[f, pad + 1 : pad + 1 + rows],
            pltpu.roll(cells, 2 * cols_here - 1, 1),
            pltpu.roll(cells, 1, 1),
        )

    empty = jnp.zeros((pad, 2 * cols_here), F32)
    for f in range(field_count + 1):
        held[f, :pad] = empty
        held[f, pad + rows :] = empty
        put_whole(f, merged[f] if f < field_count else kappa[...])

    k = held[field_count, pad : pad + rows]
    inside = k > 0.0
    coefficients = [
        jnp.where(inside, 0.5 * (k + near), 0.0) for near in neighbours_of(field_count, k)
    ]
    for sweep_index in range(SWEEPS):
        for f in range(field_count):
            u = held[f, pad : pad + rows]
            new = u
            for coefficient, near in zip(coefficients, neighbours_of(f, u), strict=True):
                new = new + coefficient * (near - u)
            if sweep_index < SWEEPS - 1:
                put(f, new)
            else:
                out[f] = new[EDGE : EDGE + rows_here, :cols_here]


def shards(
    ocean_fields,
    dest_device,
    dest_tile,
    cell_target,
    cell_weight,
    sea_mask,
    land_flux,
    land_area,
    kappa,
):
    tiles_here, field_count, tile_cells = ocean_fields.shape
    crossing_count = dest_device.shape[1]
    width_x = lax.axis_size("gx")
    width_y = lax.axis_size("gy")
    device_count = width_x * width_y
    cap = max(2, tiles_here * crossing_count * 2 // device_count)
    layer = width_x // LAYERS * width_y
    rows_here, cols_here = land_area.shape

    mirror = LAYERS // 2 * layer
    pairs = (dest_device.T, dest_tile.T, cell_target, cell_weight, sea_mask, ocean_fields)
    halves = [
        [h * (device_count // 2) + i for i in range(device_count // 2)] for h in range(2)
    ]
    exchange = functools.partial(
        lax.all_to_all,
        axis_name=("gx", "gy"),
        split_axis=0,
        concat_axis=0,
        axis_index_groups=halves,
        tiled=True,
    )
    half = device_count // 2
    everywhere = range(device_count)
    far_slots = pack(*pairs, cap, device_count, False, mirror)[0]
    pairs, far_slots = lax.optimization_barrier((pairs, far_slots))
    far_got = exchange(far_slots)
    kept, given = pack(*pairs, cap, device_count, True, 0)
    taken = lax.ppermute(given, ("gx", "gy"), [(i, i ^ 1) for i in everywhere])
    messages = join(kept, taken)

    def deliver(j):
        pairing = [(i, i ^ 2 * carried(j, i & 1)) for i in everywhere]
        if all(a != b for a, b in pairing):
            return lax.ppermute(messages[j], ("gx", "gy"), pairing)
        arrived = lax.ppermute(messages[j], ("gx", "gy"), [(a, b) for a, b in pairing if a != b])
        return jnp.where(lax.axis_index("gy") % 2 == 1, messages[j], arrived)

    soon = [deliver(j) for j in reversed(range(0, len(messages), 2))]
    late = [deliver(j) for j in range(1, len(messages), 2)]

    far_total = bin_all([far_got], [[(0, 0, half)]], [], cap, rows_here, averaged=True)[0]
    opposite = [(i, i ^ (mirror // width_y)) for i in range(width_x)]
    passed = lax.ppermute(far_total.astype(jnp.float16), "gx", opposite).astype(F32)

    def sums(messages, *which, earlier=()):
        picked = [[(j, 2 * i, 2) for j in range(len(messages))] for i in which]
        return bin_all(messages, picked, earlier, cap, rows_here)

    totals = []
    for message in soon:
        message, far_total = lax.optimization_barrier((message, far_total))
        totals = sums([message], 0, 1, earlier=totals)
        far_total = totals[0]
    own, other = totals
    for i, message in enumerate(late):
        late[i], other = lax.optimization_barrier((message, other))
        other = sums([late[i]], 1, earlier=[other])[0]
    other, passed = lax.optimization_barrier((other, passed))
    other = lax.ppermute(other, ("gx", "gy"), [(i, i ^ 1) for i in everywhere])
    own = sums(late, 0, earlier=[own])[0]

    merged, strips, edges = merge(own, other, passed, land_flux, land_area, kappa)
    before, after = neighbours(strips, "gx")
    corners = ends(select_columns(before, after))
    above, below = neighbours(jnp.concatenate([edges, corners[None]], axis=0), "gy")
    return pl.pallas_call(
        sweep_kernel,
        out_shape=jax.ShapeDtypeStruct(merged.shape, F32),
        in_specs=[VMEM] * 6,
        out_specs=VMEM,
        scratch_shapes=[
            pltpu.VMEM((field_count + 1, rows_here + 2 * EDGE + 16, 2 * cols_here), F32)
        ],
        compiler_params=params(),
    )(merged, before, after, above, below, kappa)


def solution(mesh):
    return jax.shard_map(
        shards,
        mesh=mesh,
        in_specs=(
            P(("gx", "gy"), None, None),
            P(("gx", "gy"), None),
            P(("gx", "gy"), None),
            P(("gx", "gy"), None, None),
            P(("gx", "gy"), None, None),
            P(("gx", "gy"), None),
            P(None, "gy", "gx"),
            P("gy", "gx"),
            P("gy", "gx"),
        ),
        out_specs=P(None, "gy", "gx"),
        check_vma=False,
    )
```
